32 devices in a mesh: seq: 16 (over z, y, core), tp: 2 (over x).
Axes of the slice: x: 2, y: 2, z: 4, core: 2. Of those that a mesh axis runs over, the one named last changes fastest.
Arguments:
- grad_out: bfloat16 [4096, 14336], P('seq', 'tp'), may hold values from -6 to 6
- weight: bfloat16 [4096, 14336], P('seq', 'tp'), may hold values from -0.046875 to 0.046875
- saved: bfloat16 [4096, 512], P('seq'), may hold values from -0.125 to 0.125
- first_moment: float32 [512, 14336], P('seq', 'tp'), may hold values from -6 to 6
- second_moment: float32 [512, 14336], P('seq', 'tp'), may hold values from 0.05 to 2
- basis: bfloat16 [4096, 512], P('seq'), may hold values from -0.0625 to 0.0625
- new_basis: bfloat16 [4096, 512], P('seq'), may hold values from -0.09375 to 0.09375
Outputs:
- grad_input: float32 [4096, 4096], P('seq', 'tp')
- first_new: float32 [512, 14336], P('seq', 'tp')
- second_new: float32 [512, 14336], P('seq', 'tp')
- update: float32 [512, 14336], P('seq', 'tp')
The draws below stay inside these ranges and needn't reach their ends.
All inputs are finite; a program needn't handle non-finite values.
Results may differ from the reference program's by a relative error of at most 0.0003.
Values may be sent and summed in bfloat16 or wider, within the bound.
No kernel may reach another device: no remote copies, remote signals or barrier semaphores. Data moves between devices by JAX's collectives and lax.ppermute only.
A program may use at most 192 MiB of HBM per device.

```python
import math
import jax
import jax.numpy as jnp
from jax import lax

D = 4096
F = 14336
R = 512
TOKENS = 4096


def shared_bases(key):
    first = jax.random.truncated_normal(jax.random.fold_in(key, 11), -4.0, 4.0, (D, R), jnp.float32)
    second = jax.random.truncated_normal(jax.random.fold_in(key, 12), -4.0, 4.0, (D, R), jnp.float32)
    factor = D ** (-0.5)
    return (first * factor, (0.8 * first + 0.6 * second) * factor)


def draw_basis(key, part):
    return shared_bases(key)[0].astype(jnp.bfloat16)


def draw_new_basis(key, part):
    return shared_bases(key)[1].astype(jnp.bfloat16)


def spiked(array, own_key, source, target, blocks, factor):
    def block_of(position):
        return (jnp.arange(array.shape[position]) // (array.shape[position] // blocks)).reshape((-1,) + (1,) * (array.ndim - 1 - position))

    first = jax.random.permutation(own_key, blocks)[block_of(target)]
    other_side = (block_of(target) + blocks // 2) % blocks
    return jnp.where((block_of(source) == first) | (block_of(source) == other_side), factor * array, array)


def block_scale(key, extent, pieces, low, largest):
    loudness, own = 1.0, jax.random.fold_in(key, 6)
    for dim, parts in pieces:
        heights = jnp.exp(jax.random.uniform(jax.random.fold_in(own, dim), (parts,), jnp.float32, low / len(pieces), largest / len(pieces)))
        loudness = loudness * jnp.repeat(heights, extent[dim] // parts).reshape([-1 if axis == dim else 1 for axis in range(len(extent))])
    return loudness


def bell_draw(own_key, shape, scale, bound, split=(), kind=jnp.bfloat16):
    level = block_scale(own_key, shape, split, -0.22, 0.18) if split else 1.0
    values = jax.random.normal(own_key, shape, jnp.float32) * scale * level
    return jnp.minimum(jnp.maximum(values, -bound), bound).astype(kind)


def bell_draw_with(own_key, dims, scale, reach, pieces, heavy, held_as=jnp.bfloat16):
    array = scale * jax.random.normal(own_key, dims, jnp.float32)
    if pieces:
        array = array * block_scale(own_key, dims, pieces, -0.22, 0.18)
    return jnp.clip(spiked(array, jax.random.fold_in(own_key, 3), *heavy), -reach, reach).astype(held_as)


def setup_inputs(seed: int = 0) -> dict:
    key_of = jax.random.split(jax.random.key(seed), 8)
    grad_out = bell_draw(key_of[0], (TOKENS, F), 1.0, 6.0, ((0, 16), (1, 2)))
    weight = bell_draw(key_of[1], (D, F), F ** -0.5, 0.046875, ((0, 16), (1, 2)))
    saved = bell_draw_with(key_of[2], (TOKENS, R), TOKENS ** -0.5, 0.125, ((0, 16),), (0, 1, 16, 2.0))
    first_moment = bell_draw(key_of[3], (R, F), 1.0, 6.0, ((0, 16), (1, 2)), jnp.float32)
    second_moment = jnp.clip(jnp.exp(math.log(2.0) - 3.6888794 * jax.random.uniform(key_of[4], (R, F), jnp.float32) ** block_scale(key_of[4], (R, F), ((0, 16), (1, 2)), -0.2, 0.2)), 0.05, 2.0)
    basis = draw_basis(jax.random.fold_in(key_of[7], 71), 0)
    new_basis = draw_new_basis(jax.random.fold_in(key_of[7], 71), 0)
    return dict(grad_out=grad_out, weight=weight, saved=saved, first_moment=first_moment, second_moment=second_moment, basis=basis, new_basis=new_basis)


def reference(grad_out, weight, saved, first_moment, second_moment, basis, new_basis):
    grad_input = lax.dot_general(grad_out, weight, (((1,), (1,)), ((), ())), preferred_element_type=jnp.float32)
    gradient = lax.dot_general(saved, grad_out, (((0,), (0,)), ((), ())), preferred_element_type=jnp.float32)
    intersection = lax.dot_general(new_basis, basis, (((0,), (0,)), ((), ())), preferred_element_type=jnp.float32)
    first_rot = jnp.dot(intersection, first_moment, precision=lax.Precision.HIGHEST, preferred_element_type=jnp.float32)
    second_rot = jnp.dot(intersection * intersection, second_moment, precision=lax.Precision.HIGHEST, preferred_element_type=jnp.float32)
    first_new = 0.9 * first_rot + 0.1 * gradient
    second_new = 0.95 * second_rot + 0.05 * gradient * gradient
    update = first_new / (jnp.sqrt(second_new) + 1e-08)
    return (grad_input, first_new, second_new, update)
```

```python
import jax
import jax.numpy as jnp
from jax import lax
from jax.sharding import PartitionSpec as P


def contract_rows(left, right):
    return lax.dot_general(
        left, right, (((0,), (0,)), ((), ())), preferred_element_type=jnp.float32
    )


def contract_columns(left, right):
    return lax.dot_general(
        left, right, (((1,), (1,)), ((), ())), preferred_element_type=jnp.float32
    )


def exact_dot(left, right):
    return jnp.dot(left, right, precision=lax.Precision.HIGHEST, preferred_element_type=jnp.float32)


def xor_order(items, index):
    bit = 1
    while bit < len(items):
        odd = (index & bit) != 0
        items = [jnp.where(odd, items[k ^ bit], items[k]) for k in range(len(items))]
        bit *= 2
    return items


def make_step(n, t):
    na = n // (2 * t)
    top_unit = 2 * na

    def swap(value, mask):
        return lax.ppermute(value, "seq", [(s, s ^ mask) for s in range(n)])

    def swap_tp(value, mask):
        return lax.ppermute(value, "tp", [(s, s ^ mask) for s in range(t)])

    def scatter(items, index, unit):
        items = xor_order(items, index)
        total = items[0]
        for k in range(1, len(items)):
            total = total + swap(items[k], k * unit)
        return total

    def exchange(items, index, unit):
        items = xor_order(items, index)
        return xor_order([items[0]] + [swap(items[k], k * unit) for k in range(1, len(items))], index)

    def per_device(grad_out, weight, saved, first_moment, second_moment, basis, new_basis):
        s, x = lax.axis_index("seq"), lax.axis_index("tp")
        core, group, top = s & 1, (s // 2) & (na - 1), s // top_unit
        tokens, width = grad_out.shape
        rows = first_moment.shape[0]
        half = width // 2
        part = half // na
        rank = saved.shape[1]

        w = {}
        w[0, 0] = weight
        for dz in range(1, t):
            w[dz, 0] = swap(weight, dz * top_unit)
        for dz in range(t):
            w[dz, 1] = swap(w[dz, 0], 1)

        a = [{0: grad_out[:, :half]}, {0: grad_out[:, half:]}]
        bit = na // 2
        while bit:
            for h in range(2):
                for j in list(a[h]):
                    a[h][j ^ bit] = swap(a[h][j], 2 * bit)
            bit //= 2
        saved_all = jnp.concatenate([saved if j == 0 else swap(saved, 2 * j) for j in range(na)], axis=0)

        gradient = []
        for h in range(2):
            mine = jnp.concatenate(
                [lax.dynamic_slice(a[h][j], (0, group * part), (tokens, part)) for j in range(na)], axis=0
            )
            g = contract_rows(saved_all, mine).reshape(t, na, 2, rows, part)
            g = scatter([g[:, :, 0], g[:, :, 1]], core, 1)
            g = scatter([g[k] for k in range(t)], top, top_unit)
            gradient.append(g.reshape(na * rows, part))
        gradient = jnp.concatenate(gradient, axis=1)

        local = contract_rows(new_basis, basis).reshape(t, na, 2, rows, rank)
        local = scatter([local[:, :, 0], local[:, :, 1]], core, 1)
        local = scatter([local[:, k] for k in range(na)], group, 2)
        own = scatter([local[k] for k in range(t)], top, top_unit)
        inter = jnp.stack(
            xor_order([own] + [swap(own, 2 * j) for j in range(1, na)], group), axis=0
        ).reshape(na * rows, t, na, 2, rows)
        inter = jnp.stack(xor_order([inter[:, k] for k in range(t)], top), axis=1)
        inter = jnp.stack(xor_order([inter[:, :, :, k] for k in range(2)], core), axis=2)
        inter = inter.reshape(na * rows, rank)

        def all_rows(moment):
            columns = moment.reshape(rows, 2, na, part)
            pieces = exchange([columns[:, :, k].reshape(rows, 2 * part) for k in range(na)], group, 2)
            near = jnp.concatenate(pieces, axis=0)
            found = []
            for dz in range(t):
                far = near if dz == 0 else swap(near, dz * top_unit)
                found += [far, swap(far, 1)]
            return jnp.concatenate(found, axis=0)

        first_rot = exact_dot(inter, all_rows(first_moment))
        second_rot = exact_dot(inter * inter, all_rows(second_moment))
        first = 0.9 * first_rot + 0.1 * gradient
        second = 0.95 * second_rot + 0.05 * gradient * gradient

        def own_rows(value):
            blocks = value.reshape(na, rows, 2 * part)
            pieces = exchange([blocks[k] for k in range(na)], group, 2)
            return jnp.stack([p.reshape(rows, 2, part) for p in pieces], axis=2).reshape(rows, width)

        first_new, second_new = own_rows(first), own_rows(second)
        update = first_new / (jnp.sqrt(second_new) + 1e-08)

        pieces = []
        for j in range(na):
            by_top = []
            for dz in range(t):
                c = [
                    contract_columns(a[0][j], w[dz, dc][:, :half]) + contract_columns(a[1][j], w[dz, dc][:, half:])
                    for dc in range(2)
                ]
                by_top.append(jnp.concatenate(xor_order(c, core), axis=1))
            by_top = xor_order(by_top, top ^ x)
            total = by_top[0]
            for e in range(1, t):
                total = total + swap_tp(by_top[e], e)
            pieces.append(total if j == 0 else swap(total, 2 * j))
        grad_input = jnp.concatenate(xor_order(pieces, group), axis=1)
        return (grad_input, first_new, second_new, update)

    return per_device


def solution(mesh):
    return jax.shard_map(
        make_step(mesh.shape["seq"], mesh.shape["tp"]),
        mesh=mesh,
        in_specs=(
            P("seq", "tp"),
            P("seq", "tp"),
            P("seq", None),
            P("seq", "tp"),
            P("seq", "tp"),
            P("seq", None),
            P("seq", None),
        ),
        out_specs=(P("seq", "tp"), P("seq", "tp"), P("seq", "tp"), P("seq", "tp")),
        check_vma=False,
    )
```

```python
import functools

import jax
import jax.numpy as jnp
from jax import lax
from jax.experimental import pallas as pl
from jax.experimental.pallas import tpu as pltpu
from jax.sharding import PartitionSpec as P

SCALE = 1024.0
VMEM = 40 * 2**20


def contract_rows(left, right):
    return lax.dot_general(
        left, right, (((0,), (0,)), ((), ())), preferred_element_type=jnp.float32
    )


def exact_dot(left, right):
    return jnp.dot(left, right, precision=lax.Precision.HIGHEST, preferred_element_type=jnp.float32)


def squared(value):
    return (value * jnp.abs(value) * SCALE).astype(jnp.float16)


def rooted(code):
    code = code.astype(jnp.float32) * (1.0 / SCALE)
    root = jnp.sqrt(jnp.abs(code))
    return jnp.where(code < 0, -root, root)


def xor_order(items, index):
    bit = 1
    while bit < len(items):
        odd = (index & bit) != 0
        items = [jnp.where(odd, items[k ^ bit], items[k]) for k in range(len(items))]
        bit *= 2
    return items


def together(*values):
    return lax.optimization_barrier(values)


def long_op():
    return pl.CostEstimate(flops=10**12, bytes_accessed=2**20, transcendentals=0)


def short_op():
    return pl.CostEstimate(flops=2**10, bytes_accessed=2**10, transcendentals=0)


def anchor_kernel(source, out):
    out[...] = source[...]


def anchor(value):
    return pl.pallas_call(
        anchor_kernel, out_shape=jax.ShapeDtypeStruct(value.shape, value.dtype), cost_estimate=long_op()
    )(value)


def tile_of(extent):
    return next(size for size in (512, 896, 256, 128, extent) if extent % size == 0)


def multiply_kernel(n_tokens, *refs):
    out = refs[-1]

    @pl.when(pl.program_id(0) == 0)
    def _():
        out[...] = jnp.zeros_like(out)

    left = jnp.concatenate([r[...] for r in refs[:n_tokens]], axis=0)
    right = jnp.concatenate([r[...] for r in refs[n_tokens:-1]], axis=0)
    out[...] += lax.dot_general(left, right, (((1,), (1,)), ((), ())), preferred_element_type=jnp.float32)


def multiply(tokens, rows):
    width = tokens[0].shape[1]
    tile = tile_of(width)
    height = sum(value.shape[0] for value in tokens)
    extent = sum(value.shape[0] for value in rows)
    return pl.pallas_call(
        functools.partial(multiply_kernel, len(tokens)),
        grid=(width // tile,),
        in_specs=[pl.BlockSpec((value.shape[0], tile), lambda k: (0, k)) for value in tokens + rows],
        out_specs=pl.BlockSpec((height, extent), lambda k: (0, 0)),
        out_shape=jax.ShapeDtypeStruct((height, extent), jnp.float32),
        compiler_params=pltpu.CompilerParams(vmem_limit_bytes=VMEM),
        cost_estimate=short_op(),
    )(*tokens, *rows)


def gradient_kernel(counts, place, *refs):
    keep, send = refs[-2:]
    total, at = None, len(counts)
    for saved, count in zip(refs, counts):
        block = jnp.concatenate([r[...] for r in refs[at : at + count]], axis=0)
        at += count
        product = jnp.dot(saved[...], block, preferred_element_type=jnp.float32)
        total = product if total is None else total + product
    middle = keep.shape[0]
    keep[...] = total[:middle]
    send[...] = total[middle:]


def gradient_part(saved, tokens, place, part):
    rank, depth = saved[0].shape
    if part % 128:
        total = 0.0
        for value, pieces in zip(saved, tokens):
            block = jnp.concatenate(pieces, axis=0)
            block = lax.dynamic_slice(block, (0, place * part), (depth, part))
            total = total + jnp.dot(value, block, preferred_element_type=jnp.float32)
        return total[: rank // 2], total[rank // 2 :]
    tile = part // 2 if part % 256 == 0 else part
    steps = part // tile
    flat = [value for pieces in tokens for value in pieces]
    return pl.pallas_call(
        functools.partial(gradient_kernel, [len(pieces) for pieces in tokens]),
        grid_spec=pltpu.PrefetchScalarGridSpec(
            num_scalar_prefetch=1,
            grid=(steps,),
            in_specs=[pl.BlockSpec((rank, depth), lambda i, p: (0, 0))] * len(saved)
            + [pl.BlockSpec((value.shape[0], tile), lambda i, p: (0, p[0] * steps + i)) for value in flat],
            out_specs=[pl.BlockSpec((rank // 2, tile), lambda i, p: (0, i))] * 2,
        ),
        out_shape=[jax.ShapeDtypeStruct((rank // 2, part), jnp.float32)] * 2,
        compiler_params=pltpu.CompilerParams(vmem_limit_bytes=VMEM),
        cost_estimate=short_op(),
    )(place.reshape(1), *saved, *flat)


def blend_kernel(na, group, rot_first, rot_second, gradient, *outs):
    rows = outs[0].shape[1]
    for j in range(na):
        mine = pl.ds(pl.multiple_of((group[0] ^ j) * rows, rows), rows)
        g = gradient[mine, :]
        outs[j][0] = 0.9 * rot_first[mine, :] + 0.1 * g
        outs[j][1] = 0.95 * rot_second[mine, :] + 0.05 * g * g


def blend(rot_first, rot_second, gradient, group, na):
    height, part = gradient.shape
    rows = height // na
    if rows % 8 or part % 128:
        first = 0.9 * rot_first + 0.1 * gradient
        second = 0.95 * rot_second + 0.05 * gradient * gradient
        both = jnp.stack([first, second]).reshape(2, na, rows, part)
        return xor_order([both[:, k] for k in range(na)], group)
    whole = pl.BlockSpec((height, part), lambda i, g: (0, 0))
    return pl.pallas_call(
        functools.partial(blend_kernel, na),
        grid_spec=pltpu.PrefetchScalarGridSpec(
            num_scalar_prefetch=1,
            grid=(1,),
            in_specs=[whole] * 3,
            out_specs=[pl.BlockSpec((2, rows, part), lambda i, g: (0, 0, 0))] * na,
        ),
        out_shape=[jax.ShapeDtypeStruct((2, rows, part), jnp.float32)] * na,
        compiler_params=pltpu.CompilerParams(vmem_limit_bytes=VMEM),
        cost_estimate=short_op(),
    )(group.reshape(1), rot_first, rot_second, gradient)


def finish_kernel(na, group, *refs):
    first, second, update = refs[na:]
    part = refs[0].shape[2]
    for j in range(na):
        mine = pl.ds(pl.multiple_of((group[0] ^ j) * part, 128), part)
        f, v = refs[j][0], refs[j][1]
        first[:, mine] = f
        second[:, mine] = v
        update[:, mine] = f / (jnp.sqrt(v) + 1e-08)


def finish(pieces, group):
    na = len(pieces)
    _, rows, part = pieces[0].shape
    if part % 128:
        both = jnp.concatenate(xor_order(pieces, group), axis=2)
        return both[0], both[1], both[0] / (jnp.sqrt(both[1]) + 1e-08)
    return pl.pallas_call(
        functools.partial(finish_kernel, na),
        grid_spec=pltpu.PrefetchScalarGridSpec(
            num_scalar_prefetch=1,
            grid=(1,),
            in_specs=[pl.BlockSpec((2, rows, part), lambda i, g: (0, 0, 0))] * na,
            out_specs=[pl.BlockSpec((rows, na * part), lambda i, g: (0, 0))] * 3,
        ),
        out_shape=[jax.ShapeDtypeStruct((rows, na * part), jnp.float32)] * 3,
        compiler_params=pltpu.CompilerParams(vmem_limit_bytes=VMEM),
        cost_estimate=short_op(),
    )(group.reshape(1), *pieces)


def place_kernel(na, place, *refs):
    out = refs[na]
    extent = refs[0].shape[1] // 2
    for j in range(na):
        for core in range(2):
            mine = pl.ds(pl.multiple_of((place[0] ^ (2 * j + core)) * extent, 128), extent)
            out[:, mine] = refs[j][:, core * extent : (core + 1) * extent]


def place_columns(pieces, place):
    na = len(pieces)
    tokens, extent = pieces[0].shape
    if extent % 256:
        halves = [p[:, k * extent // 2 : (k + 1) * extent // 2] for p in pieces for k in range(2)]
        return jnp.concatenate(xor_order(halves, place), axis=1)
    return pl.pallas_call(
        functools.partial(place_kernel, na),
        grid_spec=pltpu.PrefetchScalarGridSpec(
            num_scalar_prefetch=1,
            grid=(1,),
            in_specs=[pl.BlockSpec((tokens, extent), lambda i, g: (0, 0))] * na,
            out_specs=pl.BlockSpec((tokens, na * extent), lambda i, g: (0, 0)),
        ),
        out_shape=jax.ShapeDtypeStruct((tokens, na * extent), jnp.float32),
        compiler_params=pltpu.CompilerParams(vmem_limit_bytes=VMEM),
        cost_estimate=short_op(),
    )(place.reshape(1), *pieces)


def make_step(n, t):
    na = n // (2 * t)
    top_unit = 2 * na
    strides = [2**b for b in reversed(range(na.bit_length() - 1))]

    def swap(value, mask):
        return lax.ppermute(value, "seq", [(s, s ^ mask) for s in range(n)])

    def swap_tp(value, mask):
        return lax.ppermute(value, "tp", [(s, s ^ mask) for s in range(t)])

    def scatter(items, index, unit):
        items = xor_order(items, index)
        total = items[0]
        for k in range(1, len(items)):
            total = total + swap(items[k], k * unit)
        return total

    def per_device(grad_out, weight, saved, first_moment, second_moment, basis, new_basis):
        s, x = lax.axis_index("seq"), lax.axis_index("tp")
        core, group, top = s & 1, (s // 2) & (na - 1), s // top_unit
        tokens, width = grad_out.shape
        rows = first_moment.shape[0]
        part = width // na
        rank = saved.shape[1]
        drows = weight.shape[0]
        tops = range(1, t)

        def pieces_of(value):
            cuts = [0, value.shape[0] // 2, value.shape[0] * 3 // 4, value.shape[0]]
            return [value[lo:hi] for lo, hi in zip(cuts[:-1], cuts[1:])]

        last, others = strides[0], strides[1:]
        token_cuts, weight_cuts = pieces_of(grad_out), pieces_of(weight)
        a = {(0, p): token_cuts[p] for p in range(3)}
        w = {}

        def send_weight(value, p):
            for dz in tops:
                w[dz, p] = swap(value, dz * top_unit)

        def settle(p, *values):
            keys_a = [k for k in a if k[1] == p and k[0] != 0]
            keys_w = [k for k in w if k[1] == p]
            held, values = together([a[k] for k in keys_a] + [w[k] for k in keys_w], values)
            for k, v in zip(keys_a, held):
                a[k] = v
            for k, v in zip(keys_w, held[len(keys_a) :]):
                w[k] = v
            return values

        a[last, 0] = swap(token_cuts[0], 2 * last)
        send_weight(weight_cuts[0], 0)
        for bit in others:
            a[bit, 0] = swap(grad_out, 2 * bit)
        w_core = swap(weight, 1)
        ticket = anchor(jnp.full((8, 128), group, jnp.int32))
        ticket, first_moment, second_moment, new_basis, saved = together(
            ticket, first_moment, second_moment, new_basis, saved
        )

        both = squared(jnp.stack([first_moment, second_moment])).reshape(2, rows, na, part)
        near = xor_order([both[:, :, k] for k in range(na)], group)

        local = contract_rows(new_basis, basis).reshape(t, na, 2, rows, rank)
        local = scatter([local[:, :, 0], local[:, :, 1]], core, 1)
        local = xor_order([local[:, k] for k in range(na)], group)

        saved = saved.reshape(tokens, t, na, 2, rows)
        saved = jnp.stack(xor_order([saved[:, :, :, k] for k in range(2)], core), axis=1)
        saved = jnp.stack(xor_order([saved[:, :, k] for k in range(t)], top), axis=2)
        saved_t = saved.reshape(tokens, rank).T

        ticket, near, local, saved_t, more_tokens, more_weight = settle(
            0, ticket, near, local, saved_t, token_cuts[1], weight_cuts[1]
        )
        near = [near[0]] + [swap(near[j], 2 * j) for j in range(1, na)]
        local = [local[0]] + [swap(local[j], 2 * j) for j in range(1, na)]

        def forward(p):
            for bit in others:
                for j in [k[0] for k in a if k[1] == p and k[0] & last and not k[0] & bit]:
                    a[j | bit, p] = swap(a[j, p], 2 * bit)

        forward(0)
        a[last, 1] = swap(more_tokens, 2 * last)
        send_weight(more_weight, 1)
        saved_all = [saved_t if j == 0 else swap(saved_t, 2 * j) for j in range(na)]
        ticket = anchor(ticket)
        group = ticket[0, 0]
        ticket, local, near, own_rows = together(ticket, local, near, [weight, w_core])
        local = functools.reduce(jnp.add, local)
        near = jnp.concatenate(near, axis=1)
        near_other = swap(near, 1)

        ticket, local, near, more_tokens, more_weight = settle(1, ticket, local, near, token_cuts[2], weight_cuts[2])
        forward(1)
        a[last, 2] = swap(more_tokens, 2 * last)
        send_weight(more_weight, 2)
        far = {dz: swap(near, dz * top_unit) for dz in tops}
        ticket = anchor(ticket)
        group_late = ticket[0, 0]
        ticket, local = together(ticket, local)

        (ticket,) = settle(2, ticket)
        forward(2)

        def blocks_of(j):
            if j == 0:
                return [grad_out]
            return [a[j, p] for p in range(3) if (j, p) in a]

        own = scatter([local[k] for k in range(t)], top, top_unit)

        moments = [rooted(jnp.concatenate([near, near_other], axis=1))]
        for dz in tops:
            moments.append(rooted(jnp.concatenate([far[dz], swap(far[dz], 1)], axis=1)))

        inter = jnp.stack(
            xor_order([own] + [swap(own, 2 * j) for j in range(1, na)], group), axis=0
        ).reshape(na * rows, t, na, 2, rows)
        inter = xor_order([inter[:, k] for k in range(t)], top)
        rot_first = rot_second = None
        for dz in range(t):
            part_of = jnp.stack(xor_order([inter[dz][:, :, k] for k in range(2)], core), axis=1)
            part_of = jnp.stack(xor_order([part_of[:, :, k] for k in range(na)], group), axis=2)
            part_of = part_of.reshape(na * rows, 2 * na * rows)
            f = exact_dot(part_of, moments[dz][0])
            v = exact_dot(part_of * part_of, moments[dz][1])
            rot_first = f if dz == 0 else rot_first + f
            rot_second = v if dz == 0 else rot_second + v

        keep, send = gradient_part(saved_all, [blocks_of(j) for j in range(na)], group, part)
        g = (keep + swap(send, 1)).reshape(t, na * rows, part)
        gradient = g[0]
        for dz in tops:
            gradient = gradient + swap(g[dz].astype(jnp.float16), dz * top_unit).astype(jnp.float32)

        pieces = blend(rot_first, rot_second, gradient, group_late, na)
        pieces = [pieces[0]] + [swap(pieces[j], 2 * j) for j in range(1, na)]
        first_new, second_new, update = finish(pieces, group)

        other_rows = {dz: [w[dz, p] for p in range(3)] + [swap(w[dz, p], 1) for p in range(3)] for dz in tops}
        sums = [None] * na
        near_tokens = [j for j in range(na) if not j & last]
        for some in [near_tokens] + [[j] for j in range(na) if j & last]:
            block = [value for j in some for value in blocks_of(j)]
            by_top = [multiply(block, own_rows)] + [multiply(block, other_rows[dz]) for dz in tops]
            for i, j in enumerate(some):
                rel = xor_order([c[i * tokens : (i + 1) * tokens] for c in by_top], top ^ x)
                total = rel[0]
                for e in tops:
                    total = total + swap_tp(rel[e], e)
                sums[j] = swap(total, 2 * j) if j else total
        grad_input = place_columns(sums, 2 * group + core)
        return (grad_input, first_new, second_new, update)

    return per_device


def solution(mesh):
    return jax.shard_map(
        make_step(mesh.shape["seq"], mesh.shape["tp"]),
        mesh=mesh,
        in_specs=(
            P("seq", "tp"),
            P("seq", "tp"),
            P("seq", None),
            P("seq", "tp"),
            P("seq", "tp"),
            P("seq", None),
            P("seq", None),
        ),
        out_specs=(P("seq", "tp"), P("seq", "tp"), P("seq", "tp"), P("seq", "tp")),
        check_vma=False,
    )
```

```python
import functools

import jax
import jax.numpy as jnp
from jax import lax
from jax.experimental import pallas as pl
from jax.experimental.pallas import tpu as pltpu
from jax.sharding import PartitionSpec as P

SCALE = 40.0
POWER = 16
VMEM = 40 * 2**20


def contract_rows(left, right):
    return lax.dot_general(
        left, right, (((0,), (0,)), ((), ())), preferred_element_type=jnp.float32
    )


def exact_dot(left, right):
    return jnp.dot(left, right, precision=lax.Precision.HIGHEST, preferred_element_type=jnp.float32)


def powered(value):
    size = jnp.abs(value) * SCALE
    power = 1
    while power < POWER:
        size = size * size
        power *= 2
    return jnp.where(value < 0, -size, size).astype(jnp.bfloat16)


def rooted(code):
    code = code.astype(jnp.float32)
    size = jnp.abs(code)
    root = jnp.exp(jnp.log(jnp.maximum(size, 1e-38)) * (1.0 / POWER)) * (1.0 / SCALE)
    root = jnp.where(size < 1e-38, 0.0, root)
    return jnp.where(code < 0, -root, root)


def xor_order(items, index):
    bit = 1
    while bit < len(items):
        odd = (index & bit) != 0
        items = [jnp.where(odd, items[k ^ bit], items[k]) for k in range(len(items))]
        bit *= 2
    return items


def together(*values):
    return lax.optimization_barrier(values)


def long_op():
    return pl.CostEstimate(flops=10**12, bytes_accessed=2**20, transcendentals=0)


def short_op():
    return pl.CostEstimate(flops=2**10, bytes_accessed=2**10, transcendentals=0)


def anchor_kernel(source, out):
    out[...] = source[...]


def anchor(value):
    return pl.pallas_call(
        anchor_kernel, out_shape=jax.ShapeDtypeStruct(value.shape, value.dtype), cost_estimate=long_op()
    )(value)


def tile_of(extent):
    return next(size for size in (1792, 896, 512, 256, 128, extent) if extent % size == 0)


def product_of(token_refs, row_refs):
    left = jnp.concatenate([r[...] for r in token_refs], axis=0)
    right = jnp.concatenate([r[...] for r in row_refs], axis=0)
    return lax.dot_general(left, right, (((1,), (1,)), ((), ())), preferred_element_type=jnp.float32)


def multiply_kernel(n_tokens, *refs):
    out = refs[-1]

    @pl.when(pl.program_id(0) == 0)
    def _():
        out[...] = jnp.zeros_like(out)

    out[...] += product_of(refs[:n_tokens], refs[n_tokens:-1])


def multiply(tokens, rows):
    width = tokens[0].shape[1]
    tile = tile_of(width)
    height = sum(value.shape[0] for value in tokens)
    extent = sum(value.shape[0] for value in rows)
    return pl.pallas_call(
        functools.partial(multiply_kernel, len(tokens)),
        grid=(width // tile,),
        in_specs=[pl.BlockSpec((value.shape[0], tile), lambda k: (0, k)) for value in tokens + rows],
        out_specs=pl.BlockSpec((height, extent), lambda k: (0, 0)),
        out_shape=jax.ShapeDtypeStruct((height, extent), jnp.float32),
        compiler_params=pltpu.CompilerParams(vmem_limit_bytes=VMEM),
        cost_estimate=short_op(),
    )(*tokens, *rows)


def parts_kernel(n_tokens, counts, given, blocks, flag, *refs):
    t = len(counts) + given
    token_refs, at = refs[:n_tokens], n_tokens
    row_refs = []
    for count in counts:
        row_refs.append(refs[at : at + count])
        at += count
    ready = refs[at : at + given]
    at += given
    outs, sums = refs[at : at + t * blocks], refs[at + t * blocks :]
    step = pl.program_id(0)

    for total, rows in zip(sums, row_refs):
        @pl.when(step == 0)
        def _():
            total[...] = jnp.zeros_like(total)

        total[...] += product_of(token_refs, rows)

    candidates = list(ready) + list(sums)
    depth = outs[0].shape[0]

    @pl.when(step == pl.num_programs(0) - 1)
    def _():
        for f in range(t):
            @pl.when(flag[0] == f)
            def _():
                for e in range(t):
                    for j in range(blocks):
                        outs[e * blocks + j][...] = candidates[e ^ f][j * depth : (j + 1) * depth, :]


def multiply_parts(tokens, rows, flag, depth, ready=()):
    width = tokens[0].shape[1]
    tile = tile_of(width)
    height = sum(value.shape[0] for value in tokens)
    extent = sum(value.shape[0] for value in rows[0])
    blocks = height // depth
    t = len(rows) + len(ready)
    flat = [value for group in rows for value in group]
    outs = pl.pallas_call(
        functools.partial(parts_kernel, len(tokens), [len(group) for group in rows], len(ready), blocks),
        grid_spec=pltpu.PrefetchScalarGridSpec(
            num_scalar_prefetch=1,
            grid=(width // tile,),
            in_specs=[pl.BlockSpec((value.shape[0], tile), lambda k, f: (0, k)) for value in tokens + flat]
            + [pl.BlockSpec((height, extent), lambda k, f: (0, 0))] * len(ready),
            out_specs=[pl.BlockSpec((depth, extent), lambda k, f: (0, 0))] * (t * blocks),
            scratch_shapes=[pltpu.VMEM((height, extent), jnp.float32)] * len(rows),
        ),
        out_shape=[jax.ShapeDtypeStruct((depth, extent), jnp.float32)] * (t * blocks),
        compiler_params=pltpu.CompilerParams(vmem_limit_bytes=VMEM),
        cost_estimate=short_op(),
    )(flag.reshape(1), *tokens, *flat, *ready)
    return [list(outs[e * blocks : (e + 1) * blocks]) for e in range(t)]


def gradient_kernel(counts, place, *refs):
    keep, send = refs[-2:]
    total, at = None, len(counts)
    for saved, count in zip(refs, counts):
        block = jnp.concatenate([r[...] for r in refs[at : at + count]], axis=0)
        at += count
        product = jnp.dot(saved[...], block, preferred_element_type=jnp.float32)
        total = product if total is None else total + product
    middle = keep.shape[0]
    keep[...] = total[:middle]
    send[...] = total[middle:]


def gradient_part(saved, tokens, place, part):
    depth = saved[0][0].shape[1]
    rank = saved[0][0].shape[0] // saved[0][2]
    if part % 128:
        total = 0.0
        for (value, k, _), pieces in zip(saved, tokens):
            value = value[k * rank : (k + 1) * rank]
            block = jnp.concatenate(pieces, axis=0)
            block = lax.dynamic_slice(block, (0, place * part), (depth, part))
            total = total + jnp.dot(value, block, preferred_element_type=jnp.float32)
        return total[: rank // 2], total[rank // 2 :]
    tile = part // 2 if part % 256 == 0 else part
    steps = part // tile
    flat = [value for pieces in tokens for value in pieces]
    return pl.pallas_call(
        functools.partial(gradient_kernel, [len(pieces) for pieces in tokens]),
        grid_spec=pltpu.PrefetchScalarGridSpec(
            num_scalar_prefetch=1,
            grid=(steps,),
            in_specs=[pl.BlockSpec((rank, depth), lambda i, p, k=k: (k, 0)) for _, k, _ in saved]
            + [pl.BlockSpec((value.shape[0], tile), lambda i, p: (0, p[0] * steps + i)) for value in flat],
            out_specs=[pl.BlockSpec((rank // 2, tile), lambda i, p: (0, i))] * 2,
        ),
        out_shape=[jax.ShapeDtypeStruct((rank // 2, part), jnp.float32)] * 2,
        compiler_params=pltpu.CompilerParams(vmem_limit_bytes=VMEM),
        cost_estimate=short_op(),
    )(place.reshape(1), *[value for value, _, _ in saved], *flat)


def encode_kernel(na, group, first, second, *outs):
    part = outs[0].shape[2]
    for j in range(na):
        mine = pl.ds(pl.multiple_of((group[0] ^ j) * part, 128), part)
        outs[j][0] = powered(first[:, mine])
        outs[j][1] = powered(second[:, mine])


def encode(first, second, group, na):
    rows, width = first.shape
    part = width // na
    if part % 128:
        both = powered(jnp.stack([first, second])).reshape(2, rows, na, part)
        return xor_order([both[:, :, k] for k in range(na)], group)
    return list(
        pl.pallas_call(
            functools.partial(encode_kernel, na),
            grid_spec=pltpu.PrefetchScalarGridSpec(
                num_scalar_prefetch=1,
                grid=(1,),
                in_specs=[pl.BlockSpec((rows, width), lambda i, g: (0, 0))] * 2,
                out_specs=[pl.BlockSpec((2, rows, part), lambda i, g: (0, 0, 0))] * na,
            ),
            out_shape=[jax.ShapeDtypeStruct((2, rows, part), jnp.bfloat16)] * na,
            compiler_params=pltpu.CompilerParams(vmem_limit_bytes=VMEM),
            cost_estimate=short_op(),
        )(group.reshape(1), first, second)
    )


def stack_kernel(rows, *refs):
    out = refs[-1]
    for k, r in enumerate(refs[:-1]):
        out[:, k * rows : (k + 1) * rows, :] = r[...]


def stack_rows(blocks, rows):
    two, _, part = blocks[0][0].shape
    return pl.pallas_call(
        functools.partial(stack_kernel, rows),
        grid=(1,),
        in_specs=[pl.BlockSpec((two, rows, part), lambda i, k=k: (0, k, 0)) for _, k in blocks],
        out_specs=pl.BlockSpec((two, rows * len(blocks), part), lambda i: (0, 0, 0)),
        out_shape=jax.ShapeDtypeStruct((two, rows * len(blocks), part), blocks[0][0].dtype),
        compiler_params=pltpu.CompilerParams(vmem_limit_bytes=VMEM),
        cost_estimate=short_op(),
    )(*[value for value, _ in blocks])


def rotate_kernel(n_codes, inter, *refs):
    codes, (first, second) = refs[:n_codes], refs[n_codes:]
    left = inter[...]
    for k, out, matrix in ((0, first, left), (1, second, left * left)):
        moment = jnp.concatenate([rooted(c[k]) for c in codes], axis=0)
        out[...] = exact_dot(matrix, moment)


def rotate(inter, codes):
    height, rank = inter.shape
    two, rows, part = codes[0].shape
    tile = next((size for size in (896, 448, 256, 128) if part % size == 0 and size % 128 == 0), part)
    return pl.pallas_call(
        functools.partial(rotate_kernel, len(codes)),
        grid=(part // tile,),
        in_specs=[pl.BlockSpec((height, rank), lambda i: (0, 0))]
        + [pl.BlockSpec((2, rows, tile), lambda i: (0, 0, i))] * len(codes),
        out_specs=[pl.BlockSpec((height, tile), lambda i: (0, i))] * 2,
        out_shape=[jax.ShapeDtypeStruct((height, part), jnp.float32)] * 2,
        compiler_params=pltpu.CompilerParams(vmem_limit_bytes=VMEM),
        cost_estimate=short_op(),
    )(inter, *codes)


def blend_kernel(na, group, rot_first, rot_second, gradient, *outs):
    rows = outs[0].shape[1]
    for j in range(na):
        mine = pl.ds(pl.multiple_of((group[0] ^ j) * rows, rows), rows)
        g = gradient[mine, :]
        outs[j][0] = 0.9 * rot_first[mine, :] + 0.1 * g
        outs[j][1] = 0.95 * rot_second[mine, :] + 0.05 * g * g


def blend(rot_first, rot_second, gradient, group, na):
    height, part = gradient.shape
    rows = height // na
    if rows % 8 or part % 128:
        first = 0.9 * rot_first + 0.1 * gradient
        second = 0.95 * rot_second + 0.05 * gradient * gradient
        both = jnp.stack([first, second]).reshape(2, na, rows, part)
        return xor_order([both[:, k] for k in range(na)], group)
    whole = pl.BlockSpec((height, part), lambda i, g: (0, 0))
    return pl.pallas_call(
        functools.partial(blend_kernel, na),
        grid_spec=pltpu.PrefetchScalarGridSpec(
            num_scalar_prefetch=1,
            grid=(1,),
            in_specs=[whole] * 3,
            out_specs=[pl.BlockSpec((2, rows, part), lambda i, g: (0, 0, 0))] * na,
        ),
        out_shape=[jax.ShapeDtypeStruct((2, rows, part), jnp.float32)] * na,
        compiler_params=pltpu.CompilerParams(vmem_limit_bytes=VMEM),
        cost_estimate=short_op(),
    )(group.reshape(1), rot_first, rot_second, gradient)


def finish_kernel(na, group, *refs):
    first, second, update = refs[na:]
    part = refs[0].shape[2]
    for j in range(na):
        mine = pl.ds(pl.multiple_of((group[0] ^ j) * part, 128), part)
        f, v = refs[j][0], refs[j][1]
        first[:, mine] = f
        second[:, mine] = v
        update[:, mine] = f / (jnp.sqrt(v) + 1e-08)


def finish(pieces, group):
    na = len(pieces)
    _, rows, part = pieces[0].shape
    if part % 128:
        both = jnp.concatenate(xor_order(pieces, group), axis=2)
        return both[0], both[1], both[0] / (jnp.sqrt(both[1]) + 1e-08)
    return pl.pallas_call(
        functools.partial(finish_kernel, na),
        grid_spec=pltpu.PrefetchScalarGridSpec(
            num_scalar_prefetch=1,
            grid=(1,),
            in_specs=[pl.BlockSpec((2, rows, part), lambda i, g: (0, 0, 0))] * na,
            out_specs=[pl.BlockSpec((rows, na * part), lambda i, g: (0, 0))] * 3,
        ),
        out_shape=[jax.ShapeDtypeStruct((rows, na * part), jnp.float32)] * 3,
        compiler_params=pltpu.CompilerParams(vmem_limit_bytes=VMEM),
        cost_estimate=short_op(),
    )(group.reshape(1), *pieces)


def place_kernel(na, place, *refs):
    out = refs[na]
    extent = refs[0].shape[1] // 2
    for j in range(na):
        for core in range(2):
            mine = pl.ds(pl.multiple_of((place[0] ^ (2 * j + core)) * extent, 128), extent)
            out[:, mine] = refs[j][:, core * extent : (core + 1) * extent]


def place_columns(pieces, place):
    na = len(pieces)
    tokens, extent = pieces[0].shape
    if extent % 256:
        halves = [p[:, k * extent // 2 : (k + 1) * extent // 2] for p in pieces for k in range(2)]
        return jnp.concatenate(xor_order(halves, place), axis=1)
    return pl.pallas_call(
        functools.partial(place_kernel, na),
        grid_spec=pltpu.PrefetchScalarGridSpec(
            num_scalar_prefetch=1,
            grid=(1,),
            in_specs=[pl.BlockSpec((tokens, extent), lambda i, g: (0, 0))] * na,
            out_specs=pl.BlockSpec((tokens, na * extent), lambda i, g: (0, 0)),
        ),
        out_shape=jax.ShapeDtypeStruct((tokens, na * extent), jnp.float32),
        compiler_params=pltpu.CompilerParams(vmem_limit_bytes=VMEM),
        cost_estimate=short_op(),
    )(place.reshape(1), *pieces)


def make_step(n, t):
    na = n // (2 * t)
    top_unit = 2 * na
    strides = [2**b for b in reversed(range(na.bit_length() - 1))]

    def swap(value, mask):
        return lax.ppermute(value, "seq", [(s, s ^ mask) for s in range(n)])

    def swap_tp(value, mask):
        return lax.ppermute(value, "tp", [(s, s ^ mask) for s in range(t)])

    def scatter(items, index, unit):
        items = xor_order(items, index)
        total = items[0]
        for k in range(1, len(items)):
            total = total + swap(items[k], k * unit)
        return total

    def per_device(grad_out, weight, saved, first_moment, second_moment, basis, new_basis):
        s, x = lax.axis_index("seq"), lax.axis_index("tp")
        core, group, top = s & 1, (s // 2) & (na - 1), s // top_unit
        tokens, width = grad_out.shape
        rows = first_moment.shape[0]
        part = width // na
        rank = saved.shape[1]
        drows = weight.shape[0]
        tops = range(1, t)

        def pieces_of(value):
            cuts = [0, value.shape[0] // 2, value.shape[0] * 3 // 4, value.shape[0]]
            return [value[lo:hi] for lo, hi in zip(cuts[:-1], cuts[1:])]

        last, others = strides[0], strides[1:]

        def chunks_of(value):
            cuts = [0, value.shape[0] // 2, value.shape[0] * 3 // 4, value.shape[0]]
            return [value[lo:hi] for lo, hi in zip(cuts[:-1], cuts[1:])]

        token_cuts, weight_cuts = chunks_of(grad_out), chunks_of(weight)
        a, w = {}, {}

        def send(p, token_cut, weight_cut):
            a[last, p] = swap(token_cut, 2 * last)
            for dz in tops:
                w[dz, p] = swap(weight_cut, dz * top_unit)

        def forward(p):
            for bit in others:
                for j in [k[0] for k in list(a) if k[1] == p and k[0] & last and not k[0] & bit]:
                    a[j | bit, p] = swap(a[j, p], 2 * bit)

        def settle(keys_a, keys_w, *values):
            held_a, held_w, values = together([a[k] for k in keys_a], [w[k] for k in keys_w], values)
            a.update(zip(keys_a, held_a))
            w.update(zip(keys_w, held_w))
            return values

        def keys_of(p):
            return [(last, p)], [(dz, p) for dz in tops]

        def forwarded(p):
            return [k for k in a if k[1] == p and k[0] & last and k[0] != last]

        def blocks_of(j):
            return [grad_out] if j == 0 else [a[j, p] for p in range(3) if (j, p) in a]

        def hypercube(bits):
            order = [0]
            for bit in bits:
                order += [k ^ bit for k in order]
            return order

        order = hypercube(strides)

        for bit in others:
            a[bit, 0] = swap(grad_out, 2 * bit)
        send(0, token_cuts[0], weight_cuts[0])
        w_core = swap(weight, 1)
        ticket = anchor(jnp.full((8, 128), group, jnp.int32))
        ticket, first_moment, second_moment, saved, new_basis = together(
            ticket, first_moment, second_moment, saved, new_basis
        )

        local = contract_rows(new_basis, basis).reshape(t, na, 2, rows, rank)
        local = scatter([local[:, :, 0], local[:, :, 1]], core, 1)
        local = jnp.stack(xor_order([local[:, k] for k in range(na)], group))

        def halve(local, bit):
            keep, give = local[: local.shape[0] // 2], local[local.shape[0] // 2 :]
            return keep + swap(give, 2 * bit)

        local = halve(local, strides[0])

        ready = {k: [(code, 0)] for k, code in enumerate(encode(first_moment, second_moment, group, na))}

        def exchange_codes(bit):
            moving = [k for k in ready if k & bit]
            buffer = swap(stack_rows([block for k in moving for block in ready[k]], rows), 2 * bit)
            at = 0
            for k in moving:
                count = len(ready.pop(k))
                ready[k ^ bit] += [(buffer, at + m) for m in range(count)]
                at += count

        def settle_codes(*values):
            arrays = {id(block[0]): block[0] for blocks in ready.values() for block in blocks}
            held, values = together(list(arrays.values()), values)
            names = dict(zip(arrays, held))
            for k in ready:
                ready[k] = [(names[id(value)], m) for value, m in ready[k]]
            return values

        exchange_codes(strides[0])

        saved = saved.reshape(tokens, t, na, 2, rows)
        saved = jnp.stack(xor_order([saved[:, :, :, k] for k in range(2)], core), axis=1)
        saved = jnp.stack(xor_order([saved[:, :, k] for k in range(t)], top), axis=2)
        saved_all = saved.reshape(tokens, rank).T
        saved_list = [(saved_all, 0, 1)]

        spot = lax.broadcasted_iota(jnp.int32, (rank, rank), 1)
        block, within = spot // rows, spot % rows
        place = sum((block % na == k) * order[k] for k in range(na))
        source = ((block // (2 * na)) ^ top) * 2 * na + (place ^ group) * 2 + ((block // na % 2) ^ core)
        arrival = (lax.broadcasted_iota(jnp.int32, (rank, rank), 0) == source * rows + within).astype(jnp.float32)

        keys_a, keys_w = keys_of(0)
        (ticket, local, saved_all, arrival, token_cut, weight_cut, w_core) = settle_codes(
            *settle(
                keys_a + [(bit, 0) for bit in others],
                keys_w,
                ticket,
                local,
                saved_all,
                arrival,
                token_cuts[1],
                weight_cuts[1],
                w_core,
            )
        )
        for bit in others:
            exchange_codes(bit)
            local = halve(local, bit)
        forward(0)
        send(1, token_cut, weight_cut)
        ticket = anchor(ticket)
        ticket, w_core = together(ticket, w_core)
        own_rows = [weight, w_core]
        near_tokens = [j for j in range(na) if not j & last]
        far_tokens = [j for j in range(na) if j & last]
        own_products = multiply([value for j in near_tokens for value in blocks_of(j)], own_rows)
        (ticket,) = settle_codes(ticket)
        near = stack_rows(ready[0], rows)
        near_other = swap(near, 1)
        saved_list = [(saved_all, 0, 1), (swap(saved_all, 2 * last), 0, 1)]

        keys_a, keys_w = keys_of(1)
        ticket, local, near, near_other, saved_next, own_products, token_cut, weight_cut = settle(
            keys_a + forwarded(0),
            keys_w,
            ticket,
            local,
            near,
            near_other,
            saved_list[1][0],
            own_products,
            token_cuts[2],
            weight_cuts[2],
        )
        saved_list[1] = (saved_next, 0, 1)
        own = scatter([local[0, k] for k in range(t)], top, top_unit)
        forward(1)
        send(2, token_cut, weight_cut)
        for bit in others:
            both = [value[k * rank : (k + 1) * rank] for value, k, _ in saved_list]
            both = swap(jnp.concatenate(both, axis=0), 2 * bit)
            saved_list += [(both, k, len(saved_list)) for k in range(len(saved_list))]
        other_rows = {dz: [swap(w[dz, p], 1) for p in (0, 1)] for dz in tops}
        ticket = anchor(ticket)

        keys_a, keys_w = keys_of(2)
        saved_arrays = {id(value): value for value, _, _ in saved_list}
        ticket, own, near, held, other_rows = settle(
            keys_a + forwarded(1), keys_w, ticket, own, near, list(saved_arrays.values()), other_rows
        )
        names = dict(zip(saved_arrays, held))
        saved_list = [(names[id(value)], k, count) for value, k, count in saved_list]
        forward(2)
        far = {dz: swap(near, dz * top_unit) for dz in tops}
        inter = [own] + [swap(own, 2 * bit) for bit in strides[:1]]
        other_rows = [[w[dz, p] for p in range(3)] + other_rows[dz] + [swap(w[dz, 2], 1)] for dz in tops]
        ticket = anchor(ticket)

        def parts_of(js, rows_of, ready_products=()):
            blocks = [value for j in js for value in blocks_of(j)]
            flag = ticket[0, 0] ^ group ^ top ^ x
            made = multiply_parts(blocks, rows_of, flag, tokens * len(js), ready_products)
            return [m[0] for m in made]

        def over_tp(parts):
            return [swap_tp(parts[e].astype(jnp.float16), e) for e in tops]

        def total_of(parts, arrived):
            return functools.reduce(jnp.add, [parts[0]] + [value.astype(jnp.float32) for value in arrived])

        near_parts = parts_of(near_tokens, other_rows, [own_products])
        near_arrived = over_tp(near_parts)
        ticket, near_parts, inter = together(ticket, near_parts, inter)
        for bit in strides[1:]:
            inter += [swap(value, 2 * bit) for value in inter]
        inter = [inter[order.index(k)] for k in range(na)]
        all_rows = [own_rows] + other_rows
        next_parts = parts_of(far_tokens[:1], all_rows)
        next_arrived = over_tp(next_parts)

        ticket, next_parts = settle(forwarded(2), [], ticket, next_parts)
        keep, send_half = gradient_part(saved_list, [blocks_of(j) for j in order], group, part)
        ticket, keep, send_half = together(ticket, keep, send_half)
        last_parts = parts_of(far_tokens[1:], all_rows) if far_tokens[1:] else None

        (ticket, far, inter, near_arrived, near_parts, next_arrived, next_parts, last_parts, keep, send_half) = together(
            ticket, far, inter, near_arrived, near_parts, next_arrived, next_parts, last_parts, keep, send_half
        )
        got = swap(send_half, 1)
        last_arrived = over_tp(last_parts) if far_tokens[1:] else None
        far_other = {dz: swap(far[dz], 1) for dz in tops}
        g = (keep + got).reshape(t, na * rows, part)
        late_g = [swap(g[dz].astype(jnp.float16), dz * top_unit) for dz in tops]

        def go_home(js, parts, arrived):
            total = total_of(parts, arrived)
            blocks = {j: total[k * tokens : (k + 1) * tokens] for k, j in enumerate(js)}
            return {j: swap(block, 2 * j) if j else block for j, block in blocks.items()}

        sums = go_home(near_tokens, near_parts, near_arrived)
        sums.update(go_home(far_tokens[:1], next_parts, next_arrived))
        ticket = anchor(ticket)
        ticket, inter, near, near_other = together(ticket, inter, near, near_other)
        inter = exact_dot(jnp.concatenate(xor_order(inter, group), axis=0), arrival)
        codes = [near, near_other]
        for dz in tops:
            codes += [far[dz], far_other[dz]]
        rot_first, rot_second = rotate(inter, codes)

        ticket, last_arrived, sums, rot_first, rot_second = together(ticket, last_arrived, sums, rot_first, rot_second)
        if far_tokens[1:]:
            sums.update(go_home(far_tokens[1:], last_parts, last_arrived))
        ticket = anchor(ticket)
        group = ticket[0, 0]
        g, late_g, group = together(g, late_g, group)
        gradient = g[0]
        for value in late_g:
            gradient = gradient + value.astype(jnp.float32)
        pieces = blend(rot_first, rot_second, gradient, group, na)
        pieces = [pieces[0]] + [swap(pieces[j], 2 * j) for j in range(1, na)]
        grad_input = place_columns([sums[j] for j in range(na)], 2 * group + core)
        first_new, second_new, update = finish(pieces, group)
        return (grad_input, first_new, second_new, update)

    return per_device


def solution(mesh):
    return jax.shard_map(
        make_step(mesh.shape["seq"], mesh.shape["tp"]),
        mesh=mesh,
        in_specs=(
            P("seq", "tp"),
            P("seq", "tp"),
            P("seq", None),
            P("seq", "tp"),
            P("seq", "tp"),
            P("seq", None),
            P("seq", None),
        ),
        out_specs=(P("seq", "tp"), P("seq", "tp"), P("seq", "tp"), P("seq", "tp")),
        check_vma=False,
    )
```

```python
import functools

import jax
import jax.numpy as jnp
from jax import lax
from jax.experimental import pallas as pl
from jax.experimental.pallas import tpu as pltpu
from jax.sharding import PartitionSpec as P

SCALE = 40.0
POWER = 16
VMEM = 40 * 2**20


def contract_rows(left, right):
    return lax.dot_general(
        left, right, (((0,), (0,)), ((), ())), preferred_element_type=jnp.float32
    )


def exact_dot(left, right):
    return jnp.dot(left, right, precision=lax.Precision.HIGHEST, preferred_element_type=jnp.float32)


def powered(value):
    size = jnp.abs(value) * SCALE
    power = 1
    while power < POWER:
        size = size * size
        power *= 2
    return jnp.where(value < 0, -size, size).astype(jnp.bfloat16)


def rooted(code):
    code = code.astype(jnp.float32)
    size = jnp.abs(code)
    root = jnp.exp(jnp.log(jnp.maximum(size, 1e-38)) * (1.0 / POWER)) * (1.0 / SCALE)
    root = jnp.where(size < 1e-38, 0.0, root)
    return jnp.where(code < 0, -root, root)


def xor_order(items, index):
    bit = 1
    while bit < len(items):
        odd = (index & bit) != 0
        items = [jnp.where(odd, items[k ^ bit], items[k]) for k in range(len(items))]
        bit *= 2
    return items


def together(*values):
    return lax.optimization_barrier(values)


def long_op():
    return pl.CostEstimate(flops=10**12, bytes_accessed=2**20, transcendentals=0)


def short_op():
    return pl.CostEstimate(flops=2**10, bytes_accessed=2**10, transcendentals=0)


def anchor_kernel(source, out):
    out[...] = source[...]


def anchor(value, cost=long_op):
    return pl.pallas_call(
        anchor_kernel, out_shape=jax.ShapeDtypeStruct(value.shape, value.dtype), cost_estimate=cost()
    )(value)


def tile_of(extent):
    return next(size for size in (1792, 896, 512, 256, 128, extent) if extent % size == 0)


def product_of(token_refs, row_refs):
    left = jnp.concatenate([r[...] for r in token_refs], axis=0)
    right = jnp.concatenate([r[...] for r in row_refs], axis=0)
    return lax.dot_general(left, right, (((1,), (1,)), ((), ())), preferred_element_type=jnp.float32)


def multiply_kernel(n_tokens, *refs):
    out = refs[-1]

    @pl.when(pl.program_id(0) == 0)
    def _():
        out[...] = jnp.zeros_like(out)

    out[...] += product_of(refs[:n_tokens], refs[n_tokens:-1])


def multiply(tokens, rows):
    width = tokens[0].shape[1]
    tile = tile_of(width)
    height = sum(value.shape[0] for value in tokens)
    extent = sum(value.shape[0] for value in rows)
    return pl.pallas_call(
        functools.partial(multiply_kernel, len(tokens)),
        grid=(width // tile,),
        in_specs=[pl.BlockSpec((value.shape[0], tile), lambda k: (0, k)) for value in tokens + rows],
        out_specs=pl.BlockSpec((height, extent), lambda k: (0, 0)),
        out_shape=jax.ShapeDtypeStruct((height, extent), jnp.float32),
        compiler_params=pltpu.CompilerParams(vmem_limit_bytes=VMEM),
        cost_estimate=short_op(),
    )(*tokens, *rows)


def parts_kernel(n_tokens, counts, given, blocks, flag, *refs):
    t = len(counts) + given
    token_refs, at = refs[:n_tokens], n_tokens
    row_refs = []
    for count in counts:
        row_refs.append(refs[at : at + count])
        at += count
    ready = refs[at : at + given]
    at += given
    outs, sums = refs[at : at + t * blocks], refs[at + t * blocks :]
    step = pl.program_id(0)

    for total, rows in zip(sums, row_refs):
        @pl.when(step == 0)
        def _():
            total[...] = jnp.zeros_like(total)

        total[...] += product_of(token_refs, rows)

    candidates = list(ready) + list(sums)
    depth = outs[0].shape[0]

    @pl.when(step == pl.num_programs(0) - 1)
    def _():
        for f in range(t):
            @pl.when(flag[0] == f)
            def _():
                for e in range(t):
                    for j in range(blocks):
                        outs[e * blocks + j][...] = candidates[e ^ f][j * depth : (j + 1) * depth, :]


def multiply_parts(tokens, rows, flag, depth, ready=()):
    width = tokens[0].shape[1]
    tile = tile_of(width)
    height = sum(value.shape[0] for value in tokens)
    extent = sum(value.shape[0] for value in rows[0])
    blocks = height // depth
    t = len(rows) + len(ready)
    flat = [value for group in rows for value in group]
    outs = pl.pallas_call(
        functools.partial(parts_kernel, len(tokens), [len(group) for group in rows], len(ready), blocks),
        grid_spec=pltpu.PrefetchScalarGridSpec(
            num_scalar_prefetch=1,
            grid=(width // tile,),
            in_specs=[pl.BlockSpec((value.shape[0], tile), lambda k, f: (0, k)) for value in tokens + flat]
            + [pl.BlockSpec((height, extent), lambda k, f: (0, 0))] * len(ready),
            out_specs=[pl.BlockSpec((depth, extent), lambda k, f: (0, 0))] * (t * blocks),
            scratch_shapes=[pltpu.VMEM((height, extent), jnp.float32)] * len(rows),
        ),
        out_shape=[jax.ShapeDtypeStruct((depth, extent), jnp.float32)] * (t * blocks),
        compiler_params=pltpu.CompilerParams(vmem_limit_bytes=VMEM),
        cost_estimate=short_op(),
    )(flag, *tokens, *flat, *ready)
    return [list(outs[e * blocks : (e + 1) * blocks]) for e in range(t)]


def gradient_kernel(counts, place, *refs):
    keep, send = refs[-2:]
    total, at = None, len(counts)
    for saved, count in zip(refs, counts):
        block = jnp.concatenate([r[...] for r in refs[at : at + count]], axis=0)
        at += count
        product = jnp.dot(saved[...], block, preferred_element_type=jnp.float32)
        total = product if total is None else total + product
    middle = keep.shape[0]
    keep[...] = total[:middle]
    send[...] = total[middle:]


def gradient_part(saved, tokens, place, part):
    depth = saved[0][0].shape[1]
    rank = saved[0][0].shape[0] // saved[0][2]
    if part % 128:
        total = 0.0
        for (value, k, _), pieces in zip(saved, tokens):
            value = value[k * rank : (k + 1) * rank]
            block = jnp.concatenate(pieces, axis=0)
            block = lax.dynamic_slice(block, (0, place[0] * part), (depth, part))
            total = total + jnp.dot(value, block, preferred_element_type=jnp.float32)
        return total[: rank // 2], total[rank // 2 :]
    tile = part // 2 if part % 256 == 0 else part
    steps = part // tile
    flat = [value for pieces in tokens for value in pieces]
    return pl.pallas_call(
        functools.partial(gradient_kernel, [len(pieces) for pieces in tokens]),
        grid_spec=pltpu.PrefetchScalarGridSpec(
            num_scalar_prefetch=1,
            grid=(steps,),
            in_specs=[pl.BlockSpec((rank, depth), lambda i, p, k=k: (k, 0)) for _, k, _ in saved]
            + [pl.BlockSpec((value.shape[0], tile), lambda i, p: (0, p[0] * steps + i)) for value in flat],
            out_specs=[pl.BlockSpec((rank // 2, tile), lambda i, p: (0, i))] * 2,
        ),
        out_shape=[jax.ShapeDtypeStruct((rank // 2, part), jnp.float32)] * 2,
        compiler_params=pltpu.CompilerParams(vmem_limit_bytes=VMEM),
        cost_estimate=short_op(),
    )(place, *[value for value, _, _ in saved], *flat)


def encode_kernel(na, group, first, second, *outs):
    part = outs[0].shape[2]
    for j in range(na):
        mine = pl.ds(pl.multiple_of((group[0] ^ j) * part, 128), part)
        outs[j][0] = powered(first[:, mine])
        outs[j][1] = powered(second[:, mine])


def encode(first, second, group, na):
    rows, width = first.shape
    part = width // na
    if part % 128:
        both = powered(jnp.stack([first, second])).reshape(2, rows, na, part)
        return xor_order([both[:, :, k] for k in range(na)], group[0])
    return list(
        pl.pallas_call(
            functools.partial(encode_kernel, na),
            grid_spec=pltpu.PrefetchScalarGridSpec(
                num_scalar_prefetch=1,
                grid=(1,),
                in_specs=[pl.BlockSpec((rows, width), lambda i, g: (0, 0))] * 2,
                out_specs=[pl.BlockSpec((2, rows, part), lambda i, g: (0, 0, 0))] * na,
            ),
            out_shape=[jax.ShapeDtypeStruct((2, rows, part), jnp.bfloat16)] * na,
            compiler_params=pltpu.CompilerParams(vmem_limit_bytes=VMEM),
            cost_estimate=short_op(),
        )(group, first, second)
    )


def stack_kernel(rows, *refs):
    out = refs[-1]
    for k, r in enumerate(refs[:-1]):
        out[:, k * rows : (k + 1) * rows, :] = r[...]


def stack_rows(blocks, rows):
    two, _, part = blocks[0][0].shape
    return pl.pallas_call(
        functools.partial(stack_kernel, rows),
        grid=(1,),
        in_specs=[pl.BlockSpec((two, rows, part), lambda i, k=k: (0, k, 0)) for _, k in blocks],
        out_specs=pl.BlockSpec((two, rows * len(blocks), part), lambda i: (0, 0, 0)),
        out_shape=jax.ShapeDtypeStruct((two, rows * len(blocks), part), blocks[0][0].dtype),
        compiler_params=pltpu.CompilerParams(vmem_limit_bytes=VMEM),
        cost_estimate=short_op(),
    )(*[value for value, _ in blocks])


def rotate_kernel(n_codes, inter, *refs):
    codes, (first, second) = refs[:n_codes], refs[n_codes:]
    left = inter[...]
    for k, out, matrix in ((0, first, left), (1, second, left * left)):
        moment = jnp.concatenate([rooted(c[k]) for c in codes], axis=0)
        out[...] = exact_dot(matrix, moment)


def rotate(inter, codes):
    height, rank = inter.shape
    two, rows, part = codes[0].shape
    tile = next((size for size in (896, 448, 256, 128) if part % size == 0 and size % 128 == 0), part)
    return pl.pallas_call(
        functools.partial(rotate_kernel, len(codes)),
        grid=(part // tile,),
        in_specs=[pl.BlockSpec((height, rank), lambda i: (0, 0))]
        + [pl.BlockSpec((2, rows, tile), lambda i: (0, 0, i))] * len(codes),
        out_specs=[pl.BlockSpec((height, tile), lambda i: (0, i))] * 2,
        out_shape=[jax.ShapeDtypeStruct((height, part), jnp.float32)] * 2,
        compiler_params=pltpu.CompilerParams(vmem_limit_bytes=VMEM),
        cost_estimate=short_op(),
    )(inter, *codes)


def blend_kernel(na, group, rot_first, rot_second, gradient, *outs):
    rows = outs[0].shape[1]
    for j in range(na):
        mine = pl.ds(pl.multiple_of((group[0] ^ j) * rows, rows), rows)
        g = gradient[mine, :]
        outs[j][0] = 0.9 * rot_first[mine, :] + 0.1 * g
        outs[j][1] = 0.95 * rot_second[mine, :] + 0.05 * g * g


def blend(rot_first, rot_second, gradient, group, na):
    height, part = gradient.shape
    rows = height // na
    if rows % 8 or part % 128:
        first = 0.9 * rot_first + 0.1 * gradient
        second = 0.95 * rot_second + 0.05 * gradient * gradient
        both = jnp.stack([first, second]).reshape(2, na, rows, part)
        return xor_order([both[:, k] for k in range(na)], group[0])
    whole = pl.BlockSpec((height, part), lambda i, g: (0, 0))
    return pl.pallas_call(
        functools.partial(blend_kernel, na),
        grid_spec=pltpu.PrefetchScalarGridSpec(
            num_scalar_prefetch=1,
            grid=(1,),
            in_specs=[whole] * 3,
            out_specs=[pl.BlockSpec((2, rows, part), lambda i, g: (0, 0, 0))] * na,
        ),
        out_shape=[jax.ShapeDtypeStruct((2, rows, part), jnp.float32)] * na,
        compiler_params=pltpu.CompilerParams(vmem_limit_bytes=VMEM),
        cost_estimate=short_op(),
    )(group, rot_first, rot_second, gradient)


def finish_kernel(na, group, *refs):
    first, second, update = refs[na:]
    part = refs[0].shape[2]
    for j in range(na):
        mine = pl.ds(pl.multiple_of((group[0] ^ j) * part, 128), part)
        f, v = refs[j][0], refs[j][1]
        first[:, mine] = f
        second[:, mine] = v
        update[:, mine] = f / (jnp.sqrt(v) + 1e-08)


def finish(pieces, group):
    na = len(pieces)
    _, rows, part = pieces[0].shape
    if part % 128:
        both = jnp.concatenate(xor_order(pieces, group[0]), axis=2)
        return both[0], both[1], both[0] / (jnp.sqrt(both[1]) + 1e-08)
    return pl.pallas_call(
        functools.partial(finish_kernel, na),
        grid_spec=pltpu.PrefetchScalarGridSpec(
            num_scalar_prefetch=1,
            grid=(1,),
            in_specs=[pl.BlockSpec((2, rows, part), lambda i, g: (0, 0, 0))] * na,
            out_specs=[pl.BlockSpec((rows, na * part), lambda i, g: (0, 0))] * 3,
        ),
        out_shape=[jax.ShapeDtypeStruct((rows, na * part), jnp.float32)] * 3,
        compiler_params=pltpu.CompilerParams(vmem_limit_bytes=VMEM),
        cost_estimate=short_op(),
    )(group, *pieces)


def place_kernel(na, place, *refs):
    out = refs[na]
    extent = refs[0].shape[1] // 2
    for j in range(na):
        for core in range(2):
            mine = pl.ds(pl.multiple_of((place[0] ^ (2 * j + core)) * extent, 128), extent)
            out[:, mine] = refs[j][:, core * extent : (core + 1) * extent]


def place_columns(pieces, place):
    na = len(pieces)
    tokens, extent = pieces[0].shape
    if extent % 256:
        halves = [p[:, k * extent // 2 : (k + 1) * extent // 2] for p in pieces for k in range(2)]
        return jnp.concatenate(xor_order(halves, place[0]), axis=1)
    return pl.pallas_call(
        functools.partial(place_kernel, na),
        grid_spec=pltpu.PrefetchScalarGridSpec(
            num_scalar_prefetch=1,
            grid=(1,),
            in_specs=[pl.BlockSpec((tokens, extent), lambda i, g: (0, 0))] * na,
            out_specs=pl.BlockSpec((tokens, na * extent), lambda i, g: (0, 0)),
        ),
        out_shape=jax.ShapeDtypeStruct((tokens, na * extent), jnp.float32),
        compiler_params=pltpu.CompilerParams(vmem_limit_bytes=VMEM),
        cost_estimate=short_op(),
    )(place, *pieces)


def make_step(n, t):
    na = n // (2 * t)
    top_unit = 2 * na
    strides = [2**b for b in reversed(range(na.bit_length() - 1))]

    def swap(value, mask):
        return lax.ppermute(value, "seq", [(s, s ^ mask) for s in range(n)])

    def swap_tp(value, mask):
        return lax.ppermute(value, "tp", [(s, s ^ mask) for s in range(t)])

    def scatter(items, index, unit):
        items = xor_order(items, index)
        total = items[0]
        for k in range(1, len(items)):
            total = total + swap(items[k], k * unit)
        return total

    def per_device(grad_out, weight, saved, first_moment, second_moment, basis, new_basis):
        s, x = lax.axis_index("seq"), lax.axis_index("tp")
        core, group, top = s & 1, (s // 2) & (na - 1), s // top_unit
        tokens, width = grad_out.shape
        rows = first_moment.shape[0]
        part = width // na
        rank = saved.shape[1]
        drows = weight.shape[0]
        tops = range(1, t)

        last, others = strides[0], strides[1:]

        def chunks_of(value):
            cut = value.shape[0] * 5 // 8
            return [value[:cut], value[cut:]]

        token_cuts, weight_cuts = chunks_of(grad_out), chunks_of(weight)
        a, w = {}, {}

        def send(p, token_cut, weight_cut):
            a[last, p] = swap(token_cut, 2 * last)
            for dz in tops:
                w[dz, p] = swap(weight_cut, dz * top_unit)

        def forward(p):
            for bit in others:
                for j in [k[0] for k in list(a) if k[1] == p and k[0] & last and not k[0] & bit]:
                    a[j | bit, p] = swap(a[j, p], 2 * bit)

        def settle(keys_a, keys_w, *values):
            held_a, held_w, values = together([a[k] for k in keys_a], [w[k] for k in keys_w], values)
            a.update(zip(keys_a, held_a))
            w.update(zip(keys_w, held_w))
            return values

        def keys_of(p):
            return [(last, p)], [(dz, p) for dz in tops]

        def forwarded(p):
            return [k for k in a if k[1] == p and k[0] & last and k[0] != last]

        def blocks_of(j):
            return [grad_out] if j == 0 else [a[j, p] for p in range(2) if (j, p) in a]

        def hypercube(bits):
            order = [0]
            for bit in bits:
                order += [k ^ bit for k in order]
            return order

        order = hypercube(others + [last])
        at_group, flag, at_column = group.reshape(1), (top ^ x).reshape(1), (2 * group + core).reshape(1)

        for bit in others:
            a[bit, 0] = swap(grad_out, 2 * bit)
        send(0, token_cuts[0], weight_cuts[0])
        w_core = swap(weight, 1)
        ticket = jnp.full((8, 128), group, jnp.int32)

        local = contract_rows(new_basis, basis).reshape(t, na, 2, rows, rank)
        local = scatter([local[:, :, 0], local[:, :, 1]], core, 1)
        local = dict(enumerate(xor_order([local[:, k] for k in range(na)], group)))

        def halve(local, bit):
            give = [k for k in local if k & bit]
            found = swap(jnp.stack([local[k] for k in give]), 2 * bit)
            return {k ^ bit: local[k ^ bit] + found[i] for i, k in enumerate(give)}

        def exchange_codes(bit):
            moving = [k for k in ready if k & bit]
            buffer = swap(stack_rows([block for k in moving for block in ready[k]], rows), 2 * bit)
            at = 0
            for k in moving:
                count = len(ready.pop(k))
                ready[k ^ bit] += [(buffer, at + m) for m in range(count)]
                at += count

        def settle_blocks(blocks, *values):
            arrays = {id(block[0]): block[0] for block in blocks}
            held, values = together(list(arrays.values()), values)
            names = dict(zip(arrays, held))
            return [(names[id(block[0])], *block[1:]) for block in blocks], *values

        def settle_codes(*values):
            keys = [k for k in ready for _ in ready[k]]
            blocks, *values = settle_blocks([block for k in ready for block in ready[k]], *values)
            for k in ready:
                ready[k] = [block for key, block in zip(keys, blocks) if key == k]
            return values

        saved = saved.reshape(tokens, t, na, 2, rows)
        saved = jnp.stack(xor_order([saved[:, :, :, k] for k in range(2)], core), axis=1)
        saved = jnp.stack(xor_order([saved[:, :, k] for k in range(t)], top), axis=2)
        saved_list = [(saved.reshape(tokens, rank).T, 0, 1)]
        for bit in others:
            local = halve(local, bit)
        w_core, first_moment, second_moment = together(w_core, first_moment, second_moment)
        ready = {k: [(code, 0)] for k, code in enumerate(encode(first_moment, second_moment, at_group, na))}
        for bit in others:
            exchange_codes(bit)

        def exchange_saved(bit):
            both = [value[k * rank : (k + 1) * rank] for value, k, _ in saved_list]
            both = swap(jnp.concatenate(both, axis=0), 2 * bit)
            saved_list.extend([(both, k, len(saved_list)) for k in range(len(saved_list))])

        spot = lax.broadcasted_iota(jnp.int32, (rank, rank), 1)
        block, within = spot // rows, spot % rows
        place = sum((block % na == k) * order[k] for k in range(na))
        source = ((block // (2 * na)) ^ top) * 2 * na + (place ^ group) * 2 + ((block // na % 2) ^ core)
        arrival = (lax.broadcasted_iota(jnp.int32, (rank, rank), 0) == source * rows + within).astype(jnp.float32)

        keys_a, keys_w = keys_of(0)
        ticket, local, arrival, token_cut, weight_cut, w_core = settle_codes(
            *settle(
                keys_a + [(bit, 0) for bit in others],
                keys_w,
                ticket,
                local,
                arrival,
                token_cuts[1],
                weight_cuts[1],
                w_core,
            )
        )
        exchange_codes(last)
        local = halve(local, last)
        send(1, token_cut, weight_cut)
        forward(0)
        ticket = anchor(ticket)
        ticket, w_core = together(ticket, w_core)
        own_rows = [weight, w_core]
        near_tokens = [j for j in range(na) if not j & last]
        far_tokens = [j for j in range(na) if j & last]
        own_products = multiply([value for j in near_tokens for value in blocks_of(j)], own_rows)
        saved_list, ticket, local, own_products = settle_blocks(saved_list, *settle_codes(ticket, local, own_products))
        for bit in others:
            exchange_saved(bit)
        own = scatter([local[0][k] for k in range(t)], top, top_unit)
        near = stack_rows(ready[0], rows)
        saved_list, ticket, own, near = settle_blocks(saved_list, ticket, own, near)
        ticket = anchor(ticket, short_op)

        keys_a, keys_w = keys_of(1)
        ticket, own, near, own_products = settle(
            keys_a + forwarded(0), keys_w + [(dz, 0) for dz in tops], ticket, own, near, own_products
        )
        forward(1)
        far = {dz: swap(near, dz * top_unit) for dz in tops}
        inter = [own] + [swap(own, 2 * bit) for bit in strides[:1]]
        other_rows = [[w[dz, p] for p in range(2)] + [swap(w[dz, p], 1) for p in range(2)] for dz in tops]
        ticket = anchor(ticket)
        saved_list, ticket, near = settle_blocks(saved_list, ticket, near)
        exchange_saved(last)
        near_other = swap(near, 1)

        def parts_of(js, rows_of, flag, ready_products=()):
            blocks = [value for j in js for value in blocks_of(j)]
            made = multiply_parts(blocks, rows_of, flag, tokens * len(js), ready_products)
            return [m[0] for m in made]

        def over_tp(parts):
            return [swap_tp(parts[e].astype(jnp.float16), e) for e in tops]

        def total_of(parts, arrived):
            return functools.reduce(jnp.add, [parts[0]] + [value.astype(jnp.float32) for value in arrived])

        ticket, flag = together(ticket, flag)
        near_parts = parts_of(near_tokens, other_rows, flag, [own_products])
        near_arrived = over_tp(near_parts)
        ticket, near_parts, flag = together(ticket, near_parts, flag)
        all_rows = [own_rows] + other_rows
        next_parts = parts_of(far_tokens[:1], all_rows, flag)
        next_arrived = over_tp(next_parts)

        ticket, next_parts, at_group = settle(forwarded(1), [], ticket, next_parts, at_group)
        keep, send_half = gradient_part(saved_list, [blocks_of(j) for j in order], at_group, part)
        ticket, keep, send_half, flag = together(ticket, keep, send_half, flag)
        last_parts = parts_of(far_tokens[1:], all_rows, flag) if far_tokens[1:] else None

        (ticket, far, inter, near_arrived, near_parts, next_arrived, next_parts, last_parts, keep, send_half) = together(
            ticket, far, inter, near_arrived, near_parts, next_arrived, next_parts, last_parts, keep, send_half
        )
        got = swap(send_half, 1)
        last_arrived = over_tp(last_parts) if far_tokens[1:] else None
        far_other = {dz: swap(far[dz], 1) for dz in tops}
        g = (keep + got).reshape(t, na * rows, part)
        far_g = [g[dz].astype(jnp.float16) for dz in tops]
        ticket, g, far_g = together(ticket, g[0], far_g)
        late_g = [swap(value, dz * top_unit) for dz, value in zip(tops, far_g)]

        def go_home(js, parts, arrived):
            total = total_of(parts, arrived)
            blocks = {j: total[k * tokens : (k + 1) * tokens] for k, j in enumerate(js)}
            return {j: swap(block, 2 * j) if j else block for j, block in blocks.items()}

        sums = go_home(near_tokens, near_parts, near_arrived)
        sums.update(go_home(far_tokens[:1], next_parts, next_arrived))
        ticket = anchor(ticket)
        ticket, inter, near, near_other = together(ticket, inter, near, near_other)
        for bit in strides[1:]:
            inter += [swap(value, 2 * bit) for value in inter]
        inter = [inter[hypercube(strides).index(k)] for k in range(na)]
        inter = exact_dot(jnp.concatenate(xor_order(inter, group), axis=0), arrival)
        codes = [near, near_other]
        for dz in tops:
            codes += [far[dz], far_other[dz]]
        rot_first, rot_second = rotate(inter, codes)

        ticket, last_arrived, sums, rot_first, rot_second = together(ticket, last_arrived, sums, rot_first, rot_second)
        if far_tokens[1:]:
            sums.update(go_home(far_tokens[1:], last_parts, last_arrived))
        g, late_g, at_group, ticket = together(g, late_g, at_group, ticket)
        gradient = g
        for value in late_g:
            gradient = gradient + value.astype(jnp.float32)
        pieces = blend(rot_first, rot_second, gradient, at_group, na)
        pieces = [pieces[0]] + [swap(pieces[j], 2 * j) for j in range(1, na)]
        grad_input = place_columns([sums[j] for j in range(na)], at_column)
        first_new, second_new, update = finish(pieces, ticket[0, :1])
        return (grad_input, first_new, second_new, update)

    return per_device


def solution(mesh):
    return jax.shard_map(
        make_step(mesh.shape["seq"], mesh.shape["tp"]),
        mesh=mesh,
        in_specs=(
            P("seq", "tp"),
            P("seq", "tp"),
            P("seq", None),
            P("seq", "tp"),
            P("seq", "tp"),
            P("seq", None),
            P("seq", None),
        ),
        out_specs=(P("seq", "tp"), P("seq", "tp"), P("seq", "tp"), P("seq", "tp")),
        check_vma=False,
    )
```

```python
import functools

import jax
import jax.numpy as jnp
from jax import lax
from jax.experimental import pallas as pl
from jax.experimental.pallas import tpu as pltpu
from jax.sharding import PartitionSpec as P

SCALE = 40.0
POWER = 16
GRAD_BOUND = 6.0
WEIGHT_BOUND = 0.046875
VMEM = 40 * 2**20


def contract_rows(left, right):
    return lax.dot_general(
        left, right, (((0,), (0,)), ((), ())), preferred_element_type=jnp.float32
    )


def exact_dot(left, right):
    return jnp.dot(left, right, precision=lax.Precision.HIGHEST, preferred_element_type=jnp.float32)


def powered(value):
    size = jnp.abs(value) * SCALE
    power = 1
    while power < POWER:
        size = size * size
        power *= 2
    return jnp.where(value < 0, -size, size).astype(jnp.bfloat16)


def rooted(code):
    code = code.astype(jnp.float32)
    size = jnp.abs(code)
    root = jnp.exp(jnp.log(jnp.maximum(size, 1e-38)) * (1.0 / POWER)) * (1.0 / SCALE)
    root = jnp.where(size < 1e-38, 0.0, root)
    return jnp.where(code < 0, -root, root)


def sum_code(value, limit):
    size = jnp.abs(value) * (1500.0 / limit)
    size = size * size
    size = size * size
    size = size * size * size
    return jnp.where(value < 0, -size, size).astype(jnp.bfloat16)


def sum_value(code, limit):
    code = code.astype(jnp.float32)
    size = jnp.abs(code)
    root = jnp.exp(jnp.log(jnp.maximum(size, 1e-38)) * (1.0 / 12)) * (limit / 1500.0)
    root = jnp.where(size < 1e-38, 0.0, root)
    return jnp.where(code < 0, -root, root)


def xor_order(items, index):
    bit = 1
    while bit < len(items):
        odd = (index & bit) != 0
        items = [jnp.where(odd, items[k ^ bit], items[k]) for k in range(len(items))]
        bit *= 2
    return items


def together(*values):
    return lax.optimization_barrier(values)


def long_op():
    return pl.CostEstimate(flops=10**12, bytes_accessed=2**20, transcendentals=0)


def short_op():
    return pl.CostEstimate(flops=2**10, bytes_accessed=2**10, transcendentals=0)


def anchor_kernel(source, out):
    out[...] = source[...]


def anchor(value, cost=long_op):
    return pl.pallas_call(
        anchor_kernel, out_shape=jax.ShapeDtypeStruct(value.shape, value.dtype), cost_estimate=cost()
    )(value)


def tile_of(extent):
    return next(size for size in (1792, 896, 512, 256, 128, extent) if extent % size == 0)


def product_of(token_refs, row_refs):
    left = jnp.concatenate([r[...] for r in token_refs], axis=0)
    right = jnp.concatenate([r[...] for r in row_refs], axis=0)
    return lax.dot_general(left, right, (((1,), (1,)), ((), ())), preferred_element_type=jnp.float32)


def multiply_kernel(n_tokens, *refs):
    out = refs[-1]

    @pl.when(pl.program_id(0) == 0)
    def _():
        out[...] = jnp.zeros_like(out)

    out[...] += product_of(refs[:n_tokens], refs[n_tokens:-1])


def multiply(tokens, rows):
    width = tokens[0].shape[1]
    tile = tile_of(width)
    height = sum(value.shape[0] for value in tokens)
    extent = sum(value.shape[0] for value in rows)
    return pl.pallas_call(
        functools.partial(multiply_kernel, len(tokens)),
        grid=(width // tile,),
        in_specs=[pl.BlockSpec((value.shape[0], tile), lambda k: (0, k)) for value in tokens + rows],
        out_specs=pl.BlockSpec((height, extent), lambda k: (0, 0)),
        out_shape=jax.ShapeDtypeStruct((height, extent), jnp.float32),
        compiler_params=pltpu.CompilerParams(vmem_limit_bytes=VMEM),
        cost_estimate=short_op(),
    )(*tokens, *rows)


def parts_kernel(n_tokens, counts, given, blocks, limit, flag, *refs):
    t = len(counts) + given
    token_refs, at = refs[:n_tokens], n_tokens
    row_refs = []
    for count in counts:
        row_refs.append(refs[at : at + count])
        at += count
    ready = refs[at : at + given]
    at += given
    outs, sums = refs[at : at + t * blocks], refs[at + t * blocks :]
    step = pl.program_id(0)

    for total, rows in zip(sums, row_refs):
        @pl.when(step == 0)
        def _():
            total[...] = jnp.zeros_like(total)

        total[...] += product_of(token_refs, rows)

    candidates = list(ready) + list(sums)
    depth = outs[0].shape[0]

    @pl.when(step == pl.num_programs(0) - 1)
    def _():
        for f in range(t):
            @pl.when(flag[0] == f)
            def _():
                for e in range(t):
                    for j in range(blocks):
                        value = candidates[e ^ f][j * depth : (j + 1) * depth, :]
                        outs[e * blocks + j][...] = sum_code(value, limit) if e else value


def multiply_parts(tokens, rows, flag, depth, limit, ready=()):
    width = tokens[0].shape[1]
    tile = tile_of(width)
    height = sum(value.shape[0] for value in tokens)
    extent = sum(value.shape[0] for value in rows[0])
    blocks = height // depth
    t = len(rows) + len(ready)
    flat = [value for group in rows for value in group]
    outs = pl.pallas_call(
        functools.partial(parts_kernel, len(tokens), [len(group) for group in rows], len(ready), blocks, limit),
        grid_spec=pltpu.PrefetchScalarGridSpec(
            num_scalar_prefetch=1,
            grid=(width // tile,),
            in_specs=[pl.BlockSpec((value.shape[0], tile), lambda k, f: (0, k)) for value in tokens + flat]
            + [pl.BlockSpec((height, extent), lambda k, f: (0, 0))] * len(ready),
            out_specs=[pl.BlockSpec((depth, extent), lambda k, f: (0, 0))] * (t * blocks),
            scratch_shapes=[pltpu.VMEM((height, extent), jnp.float32)] * len(rows),
        ),
        out_shape=[
            jax.ShapeDtypeStruct((depth, extent), jnp.bfloat16 if e else jnp.float32)
            for e in range(t)
            for _ in range(blocks)
        ],
        compiler_params=pltpu.CompilerParams(vmem_limit_bytes=VMEM),
        cost_estimate=short_op(),
    )(flag, *tokens, *flat, *ready)
    return [list(outs[e * blocks : (e + 1) * blocks]) for e in range(t)]


def sum_kernel(n_codes, limit, keep, *refs):
    codes, outs = refs[:n_codes], refs[n_codes:]
    depth = outs[0].shape[0]
    for k, out in enumerate(outs):
        mine = slice(k * depth, (k + 1) * depth)
        total = keep[mine, :]
        for code in codes:
            total = total + sum_value(code[mine, :], limit)
        out[...] = total if out.dtype == jnp.float32 else sum_code(total, limit)


def sum_parts(keep, codes, stay, limit):
    depth = keep.shape[0] // len(stay)
    return pl.pallas_call(
        functools.partial(sum_kernel, len(codes), limit),
        out_shape=[
            jax.ShapeDtypeStruct((depth, keep.shape[1]), jnp.float32 if here else jnp.bfloat16) for here in stay
        ],
        compiler_params=pltpu.CompilerParams(vmem_limit_bytes=VMEM),
        cost_estimate=short_op(),
    )(keep, *codes)


def gradient_kernel(counts, place, *refs):
    keep, send = refs[-2:]
    total, at = None, len(counts)
    for saved, count in zip(refs, counts):
        block = jnp.concatenate([r[...] for r in refs[at : at + count]], axis=0)
        at += count
        product = jnp.dot(saved[...], block, preferred_element_type=jnp.float32)
        total = product if total is None else total + product
    middle = keep.shape[0]
    keep[...] = total[:middle]
    send[...] = total[middle:]


def gradient_part(saved, tokens, place, part):
    depth = saved[0][0].shape[1]
    rank = saved[0][0].shape[0] // saved[0][2]
    if part % 128:
        total = 0.0
        for (value, k, _), pieces in zip(saved, tokens):
            value = value[k * rank : (k + 1) * rank]
            block = jnp.concatenate(pieces, axis=0)
            block = lax.dynamic_slice(block, (0, place[0] * part), (depth, part))
            total = total + jnp.dot(value, block, preferred_element_type=jnp.float32)
        return total[: rank // 2], total[rank // 2 :]
    tile = part // 2 if part % 256 == 0 else part
    steps = part // tile
    flat = [value for pieces in tokens for value in pieces]
    return pl.pallas_call(
        functools.partial(gradient_kernel, [len(pieces) for pieces in tokens]),
        grid_spec=pltpu.PrefetchScalarGridSpec(
            num_scalar_prefetch=1,
            grid=(steps,),
            in_specs=[pl.BlockSpec((rank, depth), lambda i, p, k=k: (k, 0)) for _, k, _ in saved]
            + [pl.BlockSpec((value.shape[0], tile), lambda i, p: (0, p[0] * steps + i)) for value in flat],
            out_specs=[pl.BlockSpec((rank // 2, tile), lambda i, p: (0, i))] * 2,
        ),
        out_shape=[jax.ShapeDtypeStruct((rank // 2, part), jnp.float32)] * 2,
        compiler_params=pltpu.CompilerParams(vmem_limit_bytes=VMEM),
        cost_estimate=short_op(),
    )(place, *[value for value, _, _ in saved], *flat)


def encode_kernel(na, group, first, second, *outs):
    part = outs[0].shape[2]
    for j in range(na):
        mine = pl.ds(pl.multiple_of((group[0] ^ j) * part, 128), part)
        outs[j][0] = powered(first[:, mine])
        outs[j][1] = powered(second[:, mine])


def encode(first, second, group, na):
    rows, width = first.shape
    part = width // na
    if part % 128:
        both = powered(jnp.stack([first, second])).reshape(2, rows, na, part)
        return xor_order([both[:, :, k] for k in range(na)], group[0])
    return list(
        pl.pallas_call(
            functools.partial(encode_kernel, na),
            grid_spec=pltpu.PrefetchScalarGridSpec(
                num_scalar_prefetch=1,
                grid=(1,),
                in_specs=[pl.BlockSpec((rows, width), lambda i, g: (0, 0))] * 2,
                out_specs=[pl.BlockSpec((2, rows, part), lambda i, g: (0, 0, 0))] * na,
            ),
            out_shape=[jax.ShapeDtypeStruct((2, rows, part), jnp.bfloat16)] * na,
            compiler_params=pltpu.CompilerParams(vmem_limit_bytes=VMEM),
            cost_estimate=short_op(),
        )(group, first, second)
    )


def stack_kernel(rows, *refs):
    out = refs[-1]
    for k, r in enumerate(refs[:-1]):
        out[:, k * rows : (k + 1) * rows, :] = r[...]


def stack_rows(blocks, rows):
    two, _, part = blocks[0][0].shape
    return pl.pallas_call(
        functools.partial(stack_kernel, rows),
        grid=(1,),
        in_specs=[pl.BlockSpec((two, rows, part), lambda i, k=k: (0, k, 0)) for _, k in blocks],
        out_specs=pl.BlockSpec((two, rows * len(blocks), part), lambda i: (0, 0, 0)),
        out_shape=jax.ShapeDtypeStruct((two, rows * len(blocks), part), blocks[0][0].dtype),
        compiler_params=pltpu.CompilerParams(vmem_limit_bytes=VMEM),
        cost_estimate=short_op(),
    )(*[value for value, _ in blocks])


def rotate_kernel(n_codes, inter, *refs):
    codes, (first, second) = refs[:n_codes], refs[n_codes:]
    left = inter[...]
    for k, out, matrix in ((0, first, left), (1, second, left * left)):
        moment = jnp.concatenate([rooted(c[k]) for c in codes], axis=0)
        out[...] = exact_dot(matrix, moment)


def rotate(inter, codes):
    height, rank = inter.shape
    two, rows, part = codes[0].shape
    tile = next((size for size in (896, 448, 256, 128) if part % size == 0 and size % 128 == 0), part)
    return pl.pallas_call(
        functools.partial(rotate_kernel, len(codes)),
        grid=(part // tile,),
        in_specs=[pl.BlockSpec((height, rank), lambda i: (0, 0))]
        + [pl.BlockSpec((2, rows, tile), lambda i: (0, 0, i))] * len(codes),
        out_specs=[pl.BlockSpec((height, tile), lambda i: (0, i))] * 2,
        out_shape=[jax.ShapeDtypeStruct((height, part), jnp.float32)] * 2,
        compiler_params=pltpu.CompilerParams(vmem_limit_bytes=VMEM),
        cost_estimate=short_op(),
    )(inter, *codes)


def blend_kernel(na, group, rot_first, rot_second, gradient, *outs):
    rows = outs[0].shape[1]
    for j in range(na):
        mine = pl.ds(pl.multiple_of((group[0] ^ j) * rows, rows), rows)
        g = gradient[mine, :]
        outs[j][0] = 0.9 * rot_first[mine, :] + 0.1 * g
        outs[j][1] = 0.95 * rot_second[mine, :] + 0.05 * g * g


def blend(rot_first, rot_second, gradient, group, na):
    height, part = gradient.shape
    rows = height // na
    if rows % 8 or part % 128:
        first = 0.9 * rot_first + 0.1 * gradient
        second = 0.95 * rot_second + 0.05 * gradient * gradient
        both = jnp.stack([first, second]).reshape(2, na, rows, part)
        return xor_order([both[:, k] for k in range(na)], group[0])
    whole = pl.BlockSpec((height, part), lambda i, g: (0, 0))
    return pl.pallas_call(
        functools.partial(blend_kernel, na),
        grid_spec=pltpu.PrefetchScalarGridSpec(
            num_scalar_prefetch=1,
            grid=(1,),
            in_specs=[whole] * 3,
            out_specs=[pl.BlockSpec((2, rows, part), lambda i, g: (0, 0, 0))] * na,
        ),
        out_shape=[jax.ShapeDtypeStruct((2, rows, part), jnp.float32)] * na,
        compiler_params=pltpu.CompilerParams(vmem_limit_bytes=VMEM),
        cost_estimate=long_op(),
    )(group, rot_first, rot_second, gradient)


def finish_kernel(na, group, *refs):
    first, second, update = refs[na:]
    part = refs[0].shape[2]
    for j in range(na):
        mine = pl.ds(pl.multiple_of((group[0] ^ j) * part, 128), part)
        f, v = refs[j][0], refs[j][1]
        first[:, mine] = f
        second[:, mine] = v
        update[:, mine] = f / (jnp.sqrt(v) + 1e-08)


def finish(pieces, group):
    na = len(pieces)
    _, rows, part = pieces[0].shape
    if part % 128:
        both = jnp.concatenate(xor_order(pieces, group[0]), axis=2)
        return both[0], both[1], both[0] / (jnp.sqrt(both[1]) + 1e-08)
    return pl.pallas_call(
        functools.partial(finish_kernel, na),
        grid_spec=pltpu.PrefetchScalarGridSpec(
            num_scalar_prefetch=1,
            grid=(1,),
            in_specs=[pl.BlockSpec((2, rows, part), lambda i, g: (0, 0, 0))] * na,
            out_specs=[pl.BlockSpec((rows, na * part), lambda i, g: (0, 0))] * 3,
        ),
        out_shape=[jax.ShapeDtypeStruct((rows, na * part), jnp.float32)] * 3,
        compiler_params=pltpu.CompilerParams(vmem_limit_bytes=VMEM),
        cost_estimate=short_op(),
    )(group, *pieces)


def place_kernel(na, limit, place, *refs):
    out = refs[na]
    extent = refs[0].shape[1] // 2
    for j in range(na):
        for core in range(2):
            mine = pl.ds(pl.multiple_of((place[0] ^ (2 * j + core)) * extent, 128), extent)
            value = refs[j][:, core * extent : (core + 1) * extent]
            out[:, mine] = value if value.dtype == jnp.float32 else sum_value(value, limit)


def place_columns(pieces, place, limit):
    na = len(pieces)
    tokens, extent = pieces[0].shape
    if extent % 256:
        pieces = [p if p.dtype == jnp.float32 else sum_value(p, limit) for p in pieces]
        halves = [p[:, k * extent // 2 : (k + 1) * extent // 2] for p in pieces for k in range(2)]
        return jnp.concatenate(xor_order(halves, place[0]), axis=1)
    return pl.pallas_call(
        functools.partial(place_kernel, na, limit),
        grid_spec=pltpu.PrefetchScalarGridSpec(
            num_scalar_prefetch=1,
            grid=(1,),
            in_specs=[pl.BlockSpec((tokens, extent), lambda i, g: (0, 0))] * na,
            out_specs=pl.BlockSpec((tokens, na * extent), lambda i, g: (0, 0)),
        ),
        out_shape=jax.ShapeDtypeStruct((tokens, na * extent), jnp.float32),
        compiler_params=pltpu.CompilerParams(vmem_limit_bytes=VMEM),
        cost_estimate=short_op(),
    )(place, *pieces)


def make_step(n, t):
    na = n // (2 * t)
    top_unit = 2 * na
    strides = [2**b for b in reversed(range(na.bit_length() - 1))]

    def swap(value, mask):
        return lax.ppermute(value, "seq", [(s, s ^ mask) for s in range(n)])

    def swap_tp(value, mask):
        return lax.ppermute(value, "tp", [(s, s ^ mask) for s in range(t)])

    def scatter(items, index, unit):
        items = xor_order(items, index)
        total = items[0]
        for k in range(1, len(items)):
            total = total + swap(items[k], k * unit)
        return total

    def per_device(grad_out, weight, saved, first_moment, second_moment, basis, new_basis):
        s, x = lax.axis_index("seq"), lax.axis_index("tp")
        core, group, top = s & 1, (s // 2) & (na - 1), s // top_unit
        tokens, width = grad_out.shape
        rows = first_moment.shape[0]
        part = width // na
        rank = saved.shape[1]
        drows = weight.shape[0]
        tops = range(1, t)
        limit = GRAD_BOUND * WEIGHT_BOUND * width * t

        last, others = strides[0], strides[1:]

        def chunks_of(value):
            cut = value.shape[0] * 5 // 8
            return [value[:cut], value[cut:]]

        token_cuts, weight_cuts = chunks_of(grad_out), chunks_of(weight)
        a, w = {}, {}

        def send(p, token_cut, weight_cut):
            a[last, p] = swap(token_cut, 2 * last)
            for dz in tops:
                w[dz, p] = swap(weight_cut, dz * top_unit)

        def forward(p):
            for bit in others:
                for j in [k[0] for k in list(a) if k[1] == p and k[0] & last and not k[0] & bit]:
                    a[j | bit, p] = swap(a[j, p], 2 * bit)

        def settle(keys_a, keys_w, *values):
            held_a, held_w, values = together([a[k] for k in keys_a], [w[k] for k in keys_w], values)
            a.update(zip(keys_a, held_a))
            w.update(zip(keys_w, held_w))
            return values

        def keys_of(p):
            return [(last, p)], [(dz, p) for dz in tops]

        def forwarded(p):
            return [k for k in a if k[1] == p and k[0] & last and k[0] != last]

        def blocks_of(j):
            return [grad_out] if j == 0 else [a[j, p] for p in range(2) if (j, p) in a]

        def hypercube(bits):
            order = [0]
            for bit in bits:
                order += [k ^ bit for k in order]
            return order

        order = hypercube(others + [last])
        at_group, flag, at_column = group.reshape(1), (top ^ x).reshape(1), (2 * group + core).reshape(1)

        for bit in others:
            a[bit, 0] = swap(grad_out, 2 * bit)
        send(0, token_cuts[0], weight_cuts[0])
        w_core = swap(weight, 1)
        ticket = jnp.full((8, 128), group, jnp.int32)

        local = contract_rows(new_basis, basis).reshape(t, na, 2, rows, rank)
        local = scatter([local[:, :, 0], local[:, :, 1]], core, 1)
        local = dict(enumerate(xor_order([local[:, k] for k in range(na)], group)))

        def halve(local, bit):
            give = [k for k in local if k & bit]
            found = swap(jnp.stack([local[k] for k in give]), 2 * bit)
            return {k ^ bit: local[k ^ bit] + found[i] for i, k in enumerate(give)}

        def exchange_codes(bit):
            moving = [k for k in ready if k & bit]
            buffer = swap(stack_rows([block for k in moving for block in ready[k]], rows), 2 * bit)
            at = 0
            for k in moving:
                count = len(ready.pop(k))
                ready[k ^ bit] += [(buffer, at + m) for m in range(count)]
                at += count

        def settle_blocks(blocks, *values):
            arrays = {id(block[0]): block[0] for block in blocks}
            held, values = together(list(arrays.values()), values)
            names = dict(zip(arrays, held))
            return [(names[id(block[0])], *block[1:]) for block in blocks], *values

        def settle_codes(*values):
            keys = [k for k in ready for _ in ready[k]]
            blocks, *values = settle_blocks([block for k in ready for block in ready[k]], *values)
            for k in ready:
                ready[k] = [block for key, block in zip(keys, blocks) if key == k]
            return values

        saved = saved.reshape(tokens, t, na, 2, rows)
        saved = jnp.stack(xor_order([saved[:, :, :, k] for k in range(2)], core), axis=1)
        saved = jnp.stack(xor_order([saved[:, :, k] for k in range(t)], top), axis=2)
        saved_list = [(saved.reshape(tokens, rank).T, 0, 1)]
        for bit in others:
            local = halve(local, bit)
        w_core, first_moment, second_moment = together(w_core, first_moment, second_moment)
        ready = {k: [(code, 0)] for k, code in enumerate(encode(first_moment, second_moment, at_group, na))}
        for bit in others:
            exchange_codes(bit)

        def exchange_saved(bit):
            both = [value[k * rank : (k + 1) * rank] for value, k, _ in saved_list]
            both = swap(jnp.concatenate(both, axis=0), 2 * bit)
            saved_list.extend([(both, k, len(saved_list)) for k in range(len(saved_list))])

        spot = lax.broadcasted_iota(jnp.int32, (rank, rank), 1)
        block, within = spot // rows, spot % rows
        place = sum((block % na == k) * order[k] for k in range(na))
        source = ((block // (2 * na)) ^ top) * 2 * na + (place ^ group) * 2 + ((block // na % 2) ^ core)
        arrival = (lax.broadcasted_iota(jnp.int32, (rank, rank), 0) == source * rows + within).astype(jnp.float32)

        keys_a, keys_w = keys_of(0)
        ticket, local, arrival, token_cut, weight_cut, w_core = settle_codes(
            *settle(
                keys_a + [(bit, 0) for bit in others],
                keys_w,
                ticket,
                local,
                arrival,
                token_cuts[1],
                weight_cuts[1],
                w_core,
            )
        )
        exchange_codes(last)
        local = halve(local, last)
        send(1, token_cut, weight_cut)
        forward(0)
        ticket = anchor(ticket)
        ticket, w_core = together(ticket, w_core)
        own_rows = [weight, w_core]
        near_tokens = [j for j in range(na) if not j & last]
        far_tokens = [j for j in range(na) if j & last]
        own_products = multiply([value for j in near_tokens for value in blocks_of(j)], own_rows)
        saved_list, ticket, local, own_products = settle_blocks(saved_list, *settle_codes(ticket, local, own_products))
        for bit in others:
            exchange_saved(bit)
        own = scatter([local[0][k] for k in range(t)], top, top_unit)
        near = stack_rows(ready[0], rows)
        saved_list, ticket, own, near = settle_blocks(saved_list, ticket, own, near)
        ticket = anchor(ticket, short_op)

        keys_a, keys_w = keys_of(1)
        ticket, own, near, own_products = settle(
            keys_a + forwarded(0), keys_w + [(dz, 0) for dz in tops], ticket, own, near, own_products
        )
        forward(1)
        far = {dz: swap(near, dz * top_unit) for dz in tops}
        inter = [own] + [swap(own, 2 * bit) for bit in strides[:1]]
        other_rows = [[w[dz, p] for p in range(2)] + [swap(w[dz, p], 1) for p in range(2)] for dz in tops]
        ticket = anchor(ticket)
        saved_list, ticket, near = settle_blocks(saved_list, ticket, near)
        exchange_saved(last)
        near_other = swap(near, 1)

        def parts_of(js, rows_of, flag, ready_products=()):
            blocks = [value for j in js for value in blocks_of(j)]
            made = multiply_parts(blocks, rows_of, flag, tokens * len(js), limit, ready_products)
            return [m[0] for m in made]

        def over_tp(parts):
            return [swap_tp(parts[e], e) for e in tops]

        ticket, flag = together(ticket, flag)
        near_parts = parts_of(near_tokens, other_rows, flag, [own_products])
        near_arrived = over_tp(near_parts)
        ticket, near_parts, flag = together(ticket, near_parts, flag)
        all_rows = [own_rows] + other_rows
        next_parts = parts_of(far_tokens[:1], all_rows, flag)
        next_arrived = over_tp(next_parts)

        ticket, next_parts, at_group = settle(forwarded(1), [], ticket, next_parts, at_group)
        keep, send_half = gradient_part(saved_list, [blocks_of(j) for j in order], at_group, part)

        (ticket, far, inter, near_arrived, near_parts, next_arrived, next_parts, keep, send_half) = together(
            ticket, far, inter, near_arrived, near_parts, next_arrived, next_parts, keep, send_half
        )
        got = swap(send_half, 1)
        far_other = {dz: swap(far[dz], 1) for dz in tops}
        for bit in strides[1:]:
            found = swap(jnp.stack(inter), 2 * bit)
            inter += [found[k] for k in range(len(inter))]
        inter = [inter[hypercube(strides).index(k)] for k in range(na)]
        g = (keep + got).reshape(t, na * rows, part)
        far_g = [g[dz].astype(jnp.float16) for dz in tops]
        ticket, g, far_g = together(ticket, g[0], far_g)
        late_g = [swap(value, dz * top_unit) for dz, value in zip(tops, far_g)]
        ticket = anchor(ticket)
        ticket, near_parts, next_parts, inter = together(ticket, near_parts, next_parts, inter)

        def go_home(js, parts, arrived):
            blocks = sum_parts(parts[0], arrived, [j == 0 for j in js], limit)
            return {j: swap(block, 2 * j) if j else block for j, block in zip(js, blocks)}

        sums = go_home(near_tokens, near_parts, near_arrived)
        sums.update(go_home(far_tokens[:1], next_parts, next_arrived))
        inter = exact_dot(jnp.concatenate(xor_order(inter, group), axis=0), arrival)
        codes = [near, near_other]
        for dz in tops:
            codes += [far[dz], far_other[dz]]
        rot_first, rot_second = rotate(inter, codes)
        last_parts = []
        if far_tokens[1:]:
            rot_first, rot_second, flag = together(rot_first, rot_second, flag)
            last_parts = parts_of(far_tokens[1:], all_rows, flag)

        g, late_g, at_group, ticket, sums, last_parts = together(g, late_g, at_group, ticket, sums, last_parts)
        if far_tokens[1:]:
            last_arrived = over_tp(last_parts)
            sums.update(go_home(far_tokens[1:], last_parts, last_arrived))
        gradient = g
        for value in late_g:
            gradient = gradient + value.astype(jnp.float32)
        pieces = blend(rot_first, rot_second, gradient, at_group, na)
        pieces = [pieces[0]] + [swap(pieces[j], 2 * j) for j in range(1, na)]
        grad_input = place_columns([sums[j] for j in range(na)], at_column, limit)
        first_new, second_new, update = finish(pieces, ticket[0, :1])
        return (grad_input, first_new, second_new, update)

    return per_device


def solution(mesh):
    return jax.shard_map(
        make_step(mesh.shape["seq"], mesh.shape["tp"]),
        mesh=mesh,
        in_specs=(
            P("seq", "tp"),
            P("seq", "tp"),
            P("seq", None),
            P("seq", "tp"),
            P("seq", "tp"),
            P("seq", None),
            P("seq", None),
        ),
        out_specs=(P("seq", "tp"), P("seq", "tp"), P("seq", "tp"), P("seq", "tp")),
        check_vma=False,
    )
```

```python
import functools

import jax
import jax.numpy as jnp
from jax import lax
from jax.experimental import pallas as pl
from jax.experimental.pallas import tpu as pltpu
from jax.sharding import PartitionSpec as P

SCALE = 40.0
POWER = 16
GRAD_BOUND = 6.0
WEIGHT_BOUND = 0.046875
VMEM = 40 * 2**20


def contract_rows(left, right):
    return lax.dot_general(
        left, right, (((0,), (0,)), ((), ())), preferred_element_type=jnp.float32
    )


def exact_dot(left, right):
    return jnp.dot(left, right, precision=lax.Precision.HIGHEST, preferred_element_type=jnp.float32)


def powered(value):
    size = jnp.abs(value) * SCALE
    power = 1
    while power < POWER:
        size = size * size
        power *= 2
    return jnp.where(value < 0, -size, size).astype(jnp.bfloat16)


def rooted(code):
    code = code.astype(jnp.float32)
    size = jnp.abs(code)
    root = jnp.exp(jnp.log(jnp.maximum(size, 1e-38)) * (1.0 / POWER)) * (1.0 / SCALE)
    root = jnp.where(size < 1e-38, 0.0, root)
    return jnp.where(code < 0, -root, root)


def sum_code(value, limit):
    size = jnp.abs(value) * (1500.0 / limit)
    size = size * size
    size = size * size
    size = size * size * size
    return jnp.where(value < 0, -size, size).astype(jnp.bfloat16)


def sum_value(code, limit):
    code = code.astype(jnp.float32)
    size = jnp.abs(code)
    root = jnp.exp(jnp.log(jnp.maximum(size, 1e-38)) * (1.0 / 12)) * (limit / 1500.0)
    root = jnp.where(size < 1e-38, 0.0, root)
    return jnp.where(code < 0, -root, root)


def xor_order(items, index):
    bit = 1
    while bit < len(items):
        odd = (index & bit) != 0
        items = [jnp.where(odd, items[k ^ bit], items[k]) for k in range(len(items))]
        bit *= 2
    return items


def together(*values):
    return lax.optimization_barrier(values)


def long_op():
    return pl.CostEstimate(flops=10**12, bytes_accessed=2**20, transcendentals=0)


def short_op():
    return pl.CostEstimate(flops=2**10, bytes_accessed=2**10, transcendentals=0)


def anchor_kernel(source, out):
    out[...] = source[...]


def anchor(value, cost=long_op):
    return pl.pallas_call(
        anchor_kernel, out_shape=jax.ShapeDtypeStruct(value.shape, value.dtype), cost_estimate=cost()
    )(value)


def tile_of(extent):
    return next(size for size in (1792, 896, 512, 256, 128, extent) if extent % size == 0)


def product_of(token_refs, row_refs):
    left = jnp.concatenate([r[...] for r in token_refs], axis=0)
    right = jnp.concatenate([r[...] for r in row_refs], axis=0)
    return lax.dot_general(left, right, (((1,), (1,)), ((), ())), preferred_element_type=jnp.float32)


def multiply_kernel(n_tokens, *refs):
    out = refs[-1]

    @pl.when(pl.program_id(0) == 0)
    def _():
        out[...] = jnp.zeros_like(out)

    out[...] += product_of(refs[:n_tokens], refs[n_tokens:-1])


def multiply(tokens, rows):
    width = tokens[0].shape[1]
    tile = tile_of(width)
    height = sum(value.shape[0] for value in tokens)
    extent = sum(value.shape[0] for value in rows)
    return pl.pallas_call(
        functools.partial(multiply_kernel, len(tokens)),
        grid=(width // tile,),
        in_specs=[pl.BlockSpec((value.shape[0], tile), lambda k: (0, k)) for value in tokens + rows],
        out_specs=pl.BlockSpec((height, extent), lambda k: (0, 0)),
        out_shape=jax.ShapeDtypeStruct((height, extent), jnp.float32),
        compiler_params=pltpu.CompilerParams(vmem_limit_bytes=VMEM),
        cost_estimate=short_op(),
    )(*tokens, *rows)


def parts_kernel(n_tokens, counts, given, blocks, limit, flag, *refs):
    t = len(counts) + given
    token_refs, at = refs[:n_tokens], n_tokens
    row_refs = []
    for count in counts:
        row_refs.append(refs[at : at + count])
        at += count
    ready = refs[at : at + given]
    at += given
    outs, sums = refs[at : at + t * blocks], refs[at + t * blocks :]
    step = pl.program_id(0)

    for total, rows in zip(sums, row_refs):
        @pl.when(step == 0)
        def _():
            total[...] = jnp.zeros_like(total)

        total[...] += product_of(token_refs, rows)

    candidates = list(ready) + list(sums)
    depth = outs[0].shape[0]

    @pl.when(step == pl.num_programs(0) - 1)
    def _():
        for f in range(t):
            @pl.when(flag[0] == f)
            def _():
                for e in range(t):
                    for j in range(blocks):
                        value = candidates[e ^ f][j * depth : (j + 1) * depth, :]
                        outs[e * blocks + j][...] = sum_code(value, limit) if e else value


def multiply_parts(tokens, rows, flag, depth, limit, ready=()):
    width = tokens[0].shape[1]
    tile = tile_of(width)
    height = sum(value.shape[0] for value in tokens)
    extent = sum(value.shape[0] for value in rows[0])
    blocks = height // depth
    t = len(rows) + len(ready)
    flat = [value for group in rows for value in group]
    outs = pl.pallas_call(
        functools.partial(parts_kernel, len(tokens), [len(group) for group in rows], len(ready), blocks, limit),
        grid_spec=pltpu.PrefetchScalarGridSpec(
            num_scalar_prefetch=1,
            grid=(width // tile,),
            in_specs=[pl.BlockSpec((value.shape[0], tile), lambda k, f: (0, k)) for value in tokens + flat]
            + [pl.BlockSpec((height, extent), lambda k, f: (0, 0))] * len(ready),
            out_specs=[pl.BlockSpec((depth, extent), lambda k, f: (0, 0))] * (t * blocks),
            scratch_shapes=[pltpu.VMEM((height, extent), jnp.float32)] * len(rows),
        ),
        out_shape=[
            jax.ShapeDtypeStruct((depth, extent), jnp.bfloat16 if e else jnp.float32)
            for e in range(t)
            for _ in range(blocks)
        ],
        compiler_params=pltpu.CompilerParams(vmem_limit_bytes=VMEM),
        cost_estimate=short_op(),
    )(flag, *tokens, *flat, *ready)
    return [list(outs[e * blocks : (e + 1) * blocks]) for e in range(t)]


def sum_kernel(n_codes, limit, keep, *refs):
    codes, outs = refs[:n_codes], refs[n_codes:]
    depth = outs[0].shape[0]
    for k, out in enumerate(outs):
        mine = slice(k * depth, (k + 1) * depth)
        total = keep[mine, :]
        for code in codes:
            total = total + sum_value(code[mine, :], limit)
        out[...] = total if out.dtype == jnp.float32 else sum_code(total, limit)


def sum_parts(keep, codes, stay, limit):
    depth = keep.shape[0] // len(stay)
    return pl.pallas_call(
        functools.partial(sum_kernel, len(codes), limit),
        out_shape=[
            jax.ShapeDtypeStruct((depth, keep.shape[1]), jnp.float32 if here else jnp.bfloat16) for here in stay
        ],
        compiler_params=pltpu.CompilerParams(vmem_limit_bytes=VMEM),
        cost_estimate=short_op(),
    )(keep, *codes)


def gradient_kernel(counts, place, *refs):
    keep, send = refs[-2:]
    total, at = None, len(counts)
    for saved, count in zip(refs, counts):
        block = jnp.concatenate([r[...] for r in refs[at : at + count]], axis=0)
        at += count
        product = jnp.dot(saved[...], block, preferred_element_type=jnp.float32)
        total = product if total is None else total + product
    middle = keep.shape[0]
    keep[...] = total[:middle]
    send[...] = total[middle:]


def gradient_part(saved, tokens, place, part):
    depth = saved[0][0].shape[1]
    rank = saved[0][0].shape[0] // saved[0][2]
    if part % 128:
        total = 0.0
        for (value, k, _), pieces in zip(saved, tokens):
            value = value[k * rank : (k + 1) * rank]
            block = jnp.concatenate(pieces, axis=0)
            block = lax.dynamic_slice(block, (0, place[0] * part), (depth, part))
            total = total + jnp.dot(value, block, preferred_element_type=jnp.float32)
        return total[: rank // 2], total[rank // 2 :]
    tile = part // 2 if part % 256 == 0 else part
    steps = part // tile
    flat = [value for pieces in tokens for value in pieces]
    return pl.pallas_call(
        functools.partial(gradient_kernel, [len(pieces) for pieces in tokens]),
        grid_spec=pltpu.PrefetchScalarGridSpec(
            num_scalar_prefetch=1,
            grid=(steps,),
            in_specs=[pl.BlockSpec((rank, depth), lambda i, p, k=k: (k, 0)) for _, k, _ in saved]
            + [pl.BlockSpec((value.shape[0], tile), lambda i, p: (0, p[0] * steps + i)) for value in flat],
            out_specs=[pl.BlockSpec((rank // 2, tile), lambda i, p: (0, i))] * 2,
        ),
        out_shape=[jax.ShapeDtypeStruct((rank // 2, part), jnp.float32)] * 2,
        compiler_params=pltpu.CompilerParams(vmem_limit_bytes=VMEM),
        cost_estimate=short_op(),
    )(place, *[value for value, _, _ in saved], *flat)


def encode_kernel(na, group, first, second, *outs):
    part = outs[0].shape[2]
    for j in range(na):
        mine = pl.ds(pl.multiple_of((group[0] ^ j) * part, 128), part)
        outs[j][0] = powered(first[:, mine])
        outs[j][1] = powered(second[:, mine])


def encode(first, second, group, na):
    rows, width = first.shape
    part = width // na
    if part % 128:
        both = powered(jnp.stack([first, second])).reshape(2, rows, na, part)
        return xor_order([both[:, :, k] for k in range(na)], group[0])
    return list(
        pl.pallas_call(
            functools.partial(encode_kernel, na),
            grid_spec=pltpu.PrefetchScalarGridSpec(
                num_scalar_prefetch=1,
                grid=(1,),
                in_specs=[pl.BlockSpec((rows, width), lambda i, g: (0, 0))] * 2,
                out_specs=[pl.BlockSpec((2, rows, part), lambda i, g: (0, 0, 0))] * na,
            ),
            out_shape=[jax.ShapeDtypeStruct((2, rows, part), jnp.bfloat16)] * na,
            compiler_params=pltpu.CompilerParams(vmem_limit_bytes=VMEM),
            cost_estimate=short_op(),
        )(group, first, second)
    )


def stack_kernel(rows, *refs):
    out = refs[-1]
    for k, r in enumerate(refs[:-1]):
        out[:, k * rows : (k + 1) * rows, :] = r[...]


def stack_rows(blocks, rows):
    two, _, part = blocks[0][0].shape
    return pl.pallas_call(
        functools.partial(stack_kernel, rows),
        grid=(1,),
        in_specs=[pl.BlockSpec((two, rows, part), lambda i, k=k: (0, k, 0)) for _, k in blocks],
        out_specs=pl.BlockSpec((two, rows * len(blocks), part), lambda i: (0, 0, 0)),
        out_shape=jax.ShapeDtypeStruct((two, rows * len(blocks), part), blocks[0][0].dtype),
        compiler_params=pltpu.CompilerParams(vmem_limit_bytes=VMEM),
        cost_estimate=short_op(),
    )(*[value for value, _ in blocks])


def halves(value):
    high = value.astype(jnp.bfloat16)
    return high, (value - high.astype(jnp.float32)).astype(jnp.bfloat16)


def fine_dot(left, right):
    (a, b), (c, d) = halves(left), halves(right)

    def dot(x, y):
        return jnp.dot(x, y, preferred_element_type=jnp.float32)

    return dot(a, c) + (dot(a, d) + dot(b, c))


def rotate_kernel(n_codes, inter, *refs):
    codes, (first, second) = refs[:n_codes], refs[n_codes:]
    left = inter[...]
    for k, out, matrix in ((0, first, left), (1, second, left * left)):
        moment = jnp.concatenate([rooted(c[k]) for c in codes], axis=0)
        out[...] = fine_dot(matrix, moment)


def rotate(inter, codes):
    height, rank = inter.shape
    two, rows, part = codes[0].shape
    tile = next((size for size in (896, 448, 256, 128) if part % size == 0 and size % 128 == 0), part)
    return pl.pallas_call(
        functools.partial(rotate_kernel, len(codes)),
        grid=(part // tile,),
        in_specs=[pl.BlockSpec((height, rank), lambda i: (0, 0))]
        + [pl.BlockSpec((2, rows, tile), lambda i: (0, 0, i))] * len(codes),
        out_specs=[pl.BlockSpec((height, tile), lambda i: (0, i))] * 2,
        out_shape=[jax.ShapeDtypeStruct((height, part), jnp.float32)] * 2,
        compiler_params=pltpu.CompilerParams(vmem_limit_bytes=VMEM),
        cost_estimate=short_op(),
    )(inter, *codes)


def blend_kernel(na, group, rot_first, rot_second, gradient, *outs):
    rows = outs[0].shape[1]
    for j in range(na):
        mine = pl.ds(pl.multiple_of((group[0] ^ j) * rows, rows), rows)
        g = gradient[mine, :]
        outs[j][0] = 0.9 * rot_first[mine, :] + 0.1 * g
        outs[j][1] = 0.95 * rot_second[mine, :] + 0.05 * g * g


def blend(rot_first, rot_second, gradient, group, na):
    height, part = gradient.shape
    rows = height // na
    if rows % 8 or part % 128:
        first = 0.9 * rot_first + 0.1 * gradient
        second = 0.95 * rot_second + 0.05 * gradient * gradient
        both = jnp.stack([first, second]).reshape(2, na, rows, part)
        return xor_order([both[:, k] for k in range(na)], group[0])
    whole = pl.BlockSpec((height, part), lambda i, g: (0, 0))
    return pl.pallas_call(
        functools.partial(blend_kernel, na),
        grid_spec=pltpu.PrefetchScalarGridSpec(
            num_scalar_prefetch=1,
            grid=(1,),
            in_specs=[whole] * 3,
            out_specs=[pl.BlockSpec((2, rows, part), lambda i, g: (0, 0, 0))] * na,
        ),
        out_shape=[jax.ShapeDtypeStruct((2, rows, part), jnp.float32)] * na,
        compiler_params=pltpu.CompilerParams(vmem_limit_bytes=VMEM),
        cost_estimate=long_op(),
    )(group, rot_first, rot_second, gradient)


def finish_kernel(na, group, *refs):
    first, second, update = refs[na:]
    part = refs[0].shape[2]
    for j in range(na):
        mine = pl.ds(pl.multiple_of((group[0] ^ j) * part, 128), part)
        f, v = refs[j][0], refs[j][1]
        first[:, mine] = f
        second[:, mine] = v
        update[:, mine] = f / (jnp.sqrt(v) + 1e-08)


def finish(pieces, group):
    na = len(pieces)
    _, rows, part = pieces[0].shape
    if part % 128:
        both = jnp.concatenate(xor_order(pieces, group[0]), axis=2)
        return both[0], both[1], both[0] / (jnp.sqrt(both[1]) + 1e-08)
    return pl.pallas_call(
        functools.partial(finish_kernel, na),
        grid_spec=pltpu.PrefetchScalarGridSpec(
            num_scalar_prefetch=1,
            grid=(1,),
            in_specs=[pl.BlockSpec((2, rows, part), lambda i, g: (0, 0, 0))] * na,
            out_specs=[pl.BlockSpec((rows, na * part), lambda i, g: (0, 0))] * 3,
        ),
        out_shape=[jax.ShapeDtypeStruct((rows, na * part), jnp.float32)] * 3,
        compiler_params=pltpu.CompilerParams(vmem_limit_bytes=VMEM),
        cost_estimate=short_op(),
    )(group, *pieces)


def place_kernel(na, limit, place, *refs):
    out = refs[na]
    extent = refs[0].shape[1] // 2
    for j in range(na):
        for core in range(2):
            mine = pl.ds(pl.multiple_of((place[0] ^ (2 * j + core)) * extent, 128), extent)
            value = refs[j][:, core * extent : (core + 1) * extent]
            out[:, mine] = value if value.dtype == jnp.float32 else sum_value(value, limit)


def place_columns(pieces, place, limit):
    na = len(pieces)
    tokens, extent = pieces[0].shape
    if extent % 256:
        pieces = [p if p.dtype == jnp.float32 else sum_value(p, limit) for p in pieces]
        halves = [p[:, k * extent // 2 : (k + 1) * extent // 2] for p in pieces for k in range(2)]
        return jnp.concatenate(xor_order(halves, place[0]), axis=1)
    return pl.pallas_call(
        functools.partial(place_kernel, na, limit),
        grid_spec=pltpu.PrefetchScalarGridSpec(
            num_scalar_prefetch=1,
            grid=(1,),
            in_specs=[pl.BlockSpec((tokens, extent), lambda i, g: (0, 0))] * na,
            out_specs=pl.BlockSpec((tokens, na * extent), lambda i, g: (0, 0)),
        ),
        out_shape=jax.ShapeDtypeStruct((tokens, na * extent), jnp.float32),
        compiler_params=pltpu.CompilerParams(vmem_limit_bytes=VMEM),
        cost_estimate=short_op(),
    )(place, *pieces)


def make_step(n, t):
    na = n // (2 * t)
    top_unit = 2 * na
    strides = [2**b for b in reversed(range(na.bit_length() - 1))]

    def swap(value, mask):
        return lax.ppermute(value, "seq", [(s, s ^ mask) for s in range(n)])

    def swap_tp(value, mask):
        return lax.ppermute(value, "tp", [(s, s ^ mask) for s in range(t)])

    def scatter(items, index, unit):
        items = xor_order(items, index)
        total = items[0]
        for k in range(1, len(items)):
            total = total + swap(items[k], k * unit)
        return total

    def per_device(grad_out, weight, saved, first_moment, second_moment, basis, new_basis):
        s, x = lax.axis_index("seq"), lax.axis_index("tp")
        core, group, top = s & 1, (s // 2) & (na - 1), s // top_unit
        tokens, width = grad_out.shape
        rows = first_moment.shape[0]
        part = width // na
        rank = saved.shape[1]
        drows = weight.shape[0]
        tops = range(1, t)
        limit = GRAD_BOUND * WEIGHT_BOUND * width * t

        last, others = strides[0], strides[1:]

        def chunks_of(value):
            cut = value.shape[0] * 5 // 8
            return [value[:cut], value[cut:]]

        token_cuts, weight_cuts = chunks_of(grad_out), chunks_of(weight)
        a, w = {}, {}

        def send(p, token_cut, weight_cut):
            a[last, p] = swap(token_cut, 2 * last)
            for dz in tops:
                w[dz, p] = swap(weight_cut, dz * top_unit)

        def forward(p):
            for bit in others:
                for j in [k[0] for k in list(a) if k[1] == p and k[0] & last and not k[0] & bit]:
                    a[j | bit, p] = swap(a[j, p], 2 * bit)

        def settle(keys_a, keys_w, *values):
            held_a, held_w, values = together([a[k] for k in keys_a], [w[k] for k in keys_w], values)
            a.update(zip(keys_a, held_a))
            w.update(zip(keys_w, held_w))
            return values

        def keys_of(p):
            return [(last, p)], [(dz, p) for dz in tops]

        def forwarded(p):
            return [k for k in a if k[1] == p and k[0] & last and k[0] != last]

        def blocks_of(j):
            return [grad_out] if j == 0 else [a[j, p] for p in range(2) if (j, p) in a]

        def hypercube(bits):
            order = [0]
            for bit in bits:
                order += [k ^ bit for k in order]
            return order

        order = hypercube(others + [last])
        at_group, flag, at_column = group.reshape(1), (top ^ x).reshape(1), (2 * group + core).reshape(1)

        for bit in others:
            a[bit, 0] = swap(grad_out, 2 * bit)
        send(0, token_cuts[0], weight_cuts[0])
        w_core = swap(weight, 1)
        ticket = jnp.full((8, 128), group, jnp.int32)

        local = contract_rows(new_basis, basis).reshape(t, na, 2, rows, rank)
        local = scatter([local[:, :, 0], local[:, :, 1]], core, 1)
        local = dict(enumerate(xor_order([local[:, k] for k in range(na)], group)))

        def halve(local, bit):
            give = [k for k in local if k & bit]
            found = swap(jnp.stack([local[k] for k in give]), 2 * bit)
            return {k ^ bit: local[k ^ bit] + found[i] for i, k in enumerate(give)}

        def exchange_codes(bit):
            moving = [k for k in ready if k & bit]
            buffer = swap(stack_rows([block for k in moving for block in ready[k]], rows), 2 * bit)
            at = 0
            for k in moving:
                count = len(ready.pop(k))
                ready[k ^ bit] += [(buffer, at + m) for m in range(count)]
                at += count

        def settle_blocks(blocks, *values):
            arrays = {id(block[0]): block[0] for block in blocks}
            held, values = together(list(arrays.values()), values)
            names = dict(zip(arrays, held))
            return [(names[id(block[0])], *block[1:]) for block in blocks], *values

        def settle_codes(*values):
            keys = [k for k in ready for _ in ready[k]]
            blocks, *values = settle_blocks([block for k in ready for block in ready[k]], *values)
            for k in ready:
                ready[k] = [block for key, block in zip(keys, blocks) if key == k]
            return values

        saved = saved.reshape(tokens, t, na, 2, rows)
        saved = jnp.stack(xor_order([saved[:, :, :, k] for k in range(2)], core), axis=1)
        saved = jnp.stack(xor_order([saved[:, :, k] for k in range(t)], top), axis=2)
        saved_list = [(saved.reshape(tokens, rank).T, 0, 1)]
        for bit in others:
            local = halve(local, bit)
        w_core, first_moment, second_moment = together(w_core, first_moment, second_moment)
        ready = {k: [(code, 0)] for k, code in enumerate(encode(first_moment, second_moment, at_group, na))}
        for bit in others:
            exchange_codes(bit)

        def exchange_saved(bit):
            both = [value[k * rank : (k + 1) * rank] for value, k, _ in saved_list]
            both = swap(jnp.concatenate(both, axis=0), 2 * bit)
            saved_list.extend([(both, k, len(saved_list)) for k in range(len(saved_list))])

        spot = lax.broadcasted_iota(jnp.int32, (rank, rank), 1)
        block, within = spot // rows, spot % rows
        place = sum((block % na == k) * order[k] for k in range(na))
        source = ((block // (2 * na)) ^ top) * 2 * na + (place ^ group) * 2 + ((block // na % 2) ^ core)
        arrival = (lax.broadcasted_iota(jnp.int32, (rank, rank), 0) == source * rows + within).astype(jnp.float32)

        keys_a, keys_w = keys_of(0)
        ticket, local, arrival, token_cut, weight_cut, w_core = settle_codes(
            *settle(
                keys_a + [(bit, 0) for bit in others],
                keys_w,
                ticket,
                local,
                arrival,
                token_cuts[1],
                weight_cuts[1],
                w_core,
            )
        )
        exchange_codes(last)
        local = halve(local, last)
        send(1, token_cut, weight_cut)
        forward(0)
        ticket = anchor(ticket)
        ticket, w_core = together(ticket, w_core)
        own_rows = [weight, w_core]
        near_tokens = [j for j in range(na) if not j & last]
        far_tokens = [j for j in range(na) if j & last]
        own_products = multiply([value for j in near_tokens for value in blocks_of(j)], own_rows)
        saved_list, ticket, local, own_products = settle_blocks(saved_list, *settle_codes(ticket, local, own_products))
        for bit in others:
            exchange_saved(bit)
        own = scatter([local[0][k] for k in range(t)], top, top_unit)
        near = stack_rows(ready[0], rows)
        saved_list, ticket, own, near = settle_blocks(saved_list, ticket, own, near)
        ticket = anchor(ticket, short_op)

        keys_a, keys_w = keys_of(1)
        ticket, own, near, own_products = settle(
            keys_a + forwarded(0), keys_w + [(dz, 0) for dz in tops], ticket, own, near, own_products
        )
        forward(1)
        far = {dz: swap(near, dz * top_unit) for dz in tops}
        inter = [own] + [swap(own, 2 * bit) for bit in strides[:1]]
        other_rows = [[w[dz, p] for p in range(2)] + [swap(w[dz, p], 1) for p in range(2)] for dz in tops]
        ticket = anchor(ticket)
        saved_list, ticket, near = settle_blocks(saved_list, ticket, near)
        exchange_saved(last)
        near_other = swap(near, 1)

        def parts_of(js, rows_of, flag, ready_products=()):
            blocks = [value for j in js for value in blocks_of(j)]
            made = multiply_parts(blocks, rows_of, flag, tokens * len(js), limit, ready_products)
            return [m[0] for m in made]

        def over_tp(parts):
            return [swap_tp(parts[e], e) for e in tops]

        ticket, flag = together(ticket, flag)
        near_parts = parts_of(near_tokens, other_rows, flag, [own_products])
        near_arrived = over_tp(near_parts)
        ticket, near_parts, flag = together(ticket, near_parts, flag)
        all_rows = [own_rows] + other_rows
        next_parts = parts_of(far_tokens[:1], all_rows, flag)
        next_arrived = over_tp(next_parts)

        ticket, next_parts, at_group = settle(forwarded(1), [], ticket, next_parts, at_group)
        keep, send_half = gradient_part(saved_list, [blocks_of(j) for j in order], at_group, part)

        last_own = []
        if far_tokens[1:]:
            ticket, keep, send_half, w_core = together(ticket, keep, send_half, w_core)
            last_own = [multiply([value for j in far_tokens[1:] for value in blocks_of(j)], [weight, w_core])]
        (ticket, far, inter, near_arrived, near_parts, next_arrived, next_parts, keep, send_half, last_own) = together(
            ticket, far, inter, near_arrived, near_parts, next_arrived, next_parts, keep, send_half, last_own
        )
        got = swap(send_half, 1)
        far_other = {dz: swap(far[dz], 1) for dz in tops}
        g = (keep + got).reshape(t, na * rows, part)
        far_g = [g[dz].astype(jnp.float16) for dz in tops]
        ticket, g, far_g, inter = together(ticket, g[0], far_g, inter)
        for bit in strides[1:]:
            found = swap(jnp.stack(inter), 2 * bit)
            inter += [found[k] for k in range(len(inter))]
        inter = [inter[hypercube(strides).index(k)] for k in range(na)]
        late_g = [swap(value, dz * top_unit) for dz, value in zip(tops, far_g)]
        ticket, near_parts, next_parts, inter = together(ticket, near_parts, next_parts, inter)

        def go_home(js, parts, arrived):
            blocks = sum_parts(parts[0], arrived, [j == 0 for j in js], limit)
            return {j: swap(block, 2 * j) if j else block for j, block in zip(js, blocks)}

        sums = go_home(near_tokens, near_parts, near_arrived)
        sums.update(go_home(far_tokens[:1], next_parts, next_arrived))
        inter = exact_dot(jnp.concatenate(xor_order(inter, group), axis=0), arrival)
        codes = [near, near_other]
        for dz in tops:
            codes += [far[dz], far_other[dz]]
        rot_first, rot_second = rotate(inter, codes)
        last_parts = []
        if far_tokens[1:]:
            rot_first, rot_second, flag = together(rot_first, rot_second, flag)
            last_parts = parts_of(far_tokens[1:], other_rows, flag, last_own)

        g, late_g, at_group, ticket, sums, last_parts = together(g, late_g, at_group, ticket, sums, last_parts)
        if far_tokens[1:]:
            last_arrived = over_tp(last_parts)
            sums.update(go_home(far_tokens[1:], last_parts, last_arrived))
        gradient = g
        for value in late_g:
            gradient = gradient + value.astype(jnp.float32)
        pieces = blend(rot_first, rot_second, gradient, at_group, na)
        pieces = [pieces[0]] + [swap(pieces[j], 2 * j) for j in range(1, na)]
        grad_input = place_columns([sums[j] for j in range(na)], at_column, limit)
        first_new, second_new, update = finish(pieces, ticket[0, :1])
        return (grad_input, first_new, second_new, update)

    return per_device


def solution(mesh):
    return jax.shard_map(
        make_step(mesh.shape["seq"], mesh.shape["tp"]),
        mesh=mesh,
        in_specs=(
            P("seq", "tp"),
            P("seq", "tp"),
            P("seq", None),
            P("seq", "tp"),
            P("seq", "tp"),
            P("seq", None),
            P("seq", None),
        ),
        out_specs=(P("seq", "tp"), P("seq", "tp"), P("seq", "tp"), P("seq", "tp")),
        check_vma=False,
    )
```
